1024 devices in a mesh: rep: 16 (over z, x_lo), fsdp: 64 (over y, x_hi, core).
Axes of the slice: x: 8 (x_hi: 4, x_lo: 2; x = x_hi * 2 + x_lo), y: 8, z: 8, core: 2. Of those that a mesh axis runs over, the one named last changes fastest.
Arguments:
- tokens_in: bfloat16 [16, 8192, 8192], P('rep', 'fsdp'), may hold values from -16 to 16
- norm_gain: bfloat16 [16, 8192], P('rep', 'fsdp'), may hold values from 0.099609375 to 1.8984375
- value_weight: bfloat16 [16, 8192, 128], P('rep', 'fsdp'), may hold values from -0.0625 to 0.0625
- value_cotangent: bfloat16 [16, 8192, 128], P('rep', 'fsdp'), may hold values from -6 to 6
- step_count: int32 [], replicated, may hold values from 1 to 8
- m_weight: float32 [16, 8192, 128], P('rep', 'fsdp'), may hold values from -0.15625 to 0.15625
- v_weight: float32 [16, 8192, 128], P('rep', 'fsdp'), may hold values from 3.6621095e-05 to 0.00036621094
- m_gain: float32 [16, 8192], P('rep', 'fsdp'), may hold values from -0.01953125 to 0.01953125
- v_gain: float32 [16, 8192], P('rep', 'fsdp'), may hold values from 5.722046e-07 to 5.722046e-06
- frag_local: float32 [16, 8192, 1024], P('rep', 'fsdp'), may hold values from -6 to 6
- frag_global: float32 [8192, 1024], P('fsdp'), may hold values from -6 to 6
- frag_moment: float32 [8192, 1024], P('fsdp'), may hold values from -4 to 4
Outputs:
- values: bfloat16 [16, 8192, 128], P('rep', 'fsdp')
- weight_step: float32 [16, 8192, 128], P('rep', 'fsdp')
- gain_step: float32 [16, 8192], P('rep', 'fsdp')
- new_global: float32 [8192, 1024], P('fsdp')
- new_moment: float32 [8192, 1024], P('fsdp')
The draws below stay inside these ranges and needn't reach their ends.
All inputs are finite; a program needn't handle non-finite values.
Results may differ from the reference program's by a relative error of at most 0.015.
Values may be sent and summed in bfloat16 or wider, within the bound.
No kernel may reach another device: no remote copies, remote signals or barrier semaphores. Data moves between devices by JAX's collectives and lax.ppermute only.
A program may use at most 32 MiB of HBM per device.

```python
import math
import jax
import jax.numpy as jnp
from jax import lax

D = 8192
HEAD = 128
FRAG = 1024
TOKENS = 8192
REPLICAS = 16


def raised(result, own_key, source, target, parts, factor):
    owner, partner = [(jnp.arange(result.shape[axis_at]) // (result.shape[axis_at] // parts)).reshape([-1 if axis == axis_at else 1 for axis in range(result.ndim)]) for axis_at in (source, target)]
    chosen = jax.random.permutation(own_key, parts)[partner]
    strong = (owner == chosen) | (owner == (partner + parts // 2) % parts)
    return jnp.where(strong, factor * result, result)


def level_of(stream_key, extent, split, smallest, top_value):
    def one(dim, parts):
        draws = jax.random.uniform(jax.random.fold_in(jax.random.fold_in(stream_key, 6), dim), (parts,), jnp.float32, smallest / len(split), top_value / len(split))
        return jnp.repeat(jnp.exp(draws), extent[dim] // parts).reshape((-1,) + (1,) * (len(extent) - dim - 1))

    loudness = one(*split[0])
    for cut in split[1:]:
        loudness = loudness * one(*cut)
    return loudness


def centred(stream_key, extent, scale, bound, pieces=(), held_as=jnp.bfloat16):
    array = scale * jax.random.normal(stream_key, extent, jnp.float32)
    if pieces:
        array = array * level_of(stream_key, extent, pieces, -0.22, 0.18)
    return jnp.clip(array, -bound, bound).astype(held_as)


def gaussian_with(own_key, extent, scale, reach, split, heavy, kind=jnp.bfloat16):
    drawn = scale * jax.random.normal(own_key, extent, jnp.float32)
    if split:
        drawn = drawn * level_of(own_key, extent, split, -0.22, 0.18)
    return jnp.clip(raised(drawn, jax.random.fold_in(own_key, 3), *heavy), -reach, reach).astype(kind)


def setup_inputs(seed: int = 0) -> dict:
    key_of = jax.random.split(jax.random.key(seed), 13)
    tokens_in = gaussian_with(key_of[0], (REPLICAS, TOKENS, D), 1.0, 16.0, ((0, 16), (1, 64)), (1, 2, 64, 4.0))
    norm_gain = jnp.clip(1.0 + 0.18 * jax.random.normal(key_of[1], (REPLICAS, D), jnp.float32), 0.099609375, 1.8984375).astype(jnp.bfloat16)
    value_weight = centred(key_of[2], (REPLICAS, D, HEAD), D ** -0.5, 0.0625, ((0, 16), (1, 64)))
    value_cotangent = centred(key_of[3], (REPLICAS, TOKENS, HEAD), 1.0, 6.0, ((0, 16), (1, 64)))
    step_count = jax.random.randint(key_of[4], (), 1, 9).astype(jnp.int32)
    m_weight = centred(key_of[5], (REPLICAS, D, HEAD), (TOKENS ** -0.5), 0.15625, ((0, 16), (1, 64)), jnp.float32)
    v_weight = jnp.clip(jnp.exp(math.log(0.00036621094) - 2.3025851 * jax.random.uniform(key_of[6], (REPLICAS, D, HEAD), jnp.float32) ** level_of(key_of[6], (REPLICAS, D, HEAD), ((0, 16), (1, 64)), -0.2, 0.2)), 3.662109520519152e-05, 0.00036621094)
    m_gain = centred(key_of[7], (REPLICAS, D), ((HEAD / D / TOKENS) ** 0.5), 0.01953125, ((0, 16), (1, 64)), jnp.float32)
    v_gain = jnp.clip(jnp.exp(math.log(5.7220458984375e-06) - 2.3025851 * jax.random.uniform(key_of[8], (REPLICAS, D), jnp.float32) ** level_of(key_of[8], (REPLICAS, D), ((0, 16), (1, 64)), -0.2, 0.2)), 5.722046125811175e-07, 5.7220458984375e-06)
    frag_local = centred(key_of[9], (REPLICAS, D, FRAG), 1.0, 6.0, ((0, 16), (1, 64)), jnp.float32)
    frag_global = centred(key_of[10], (D, FRAG), 1.0, 6.0, ((0, 64),), jnp.float32)
    frag_moment = centred(key_of[11], (D, FRAG), 0.5, 4.0, ((0, 64),), jnp.float32)
    return dict(tokens_in=tokens_in, norm_gain=norm_gain, value_weight=value_weight, value_cotangent=value_cotangent, step_count=step_count, m_weight=m_weight, v_weight=v_weight, m_gain=m_gain, v_gain=v_gain, frag_local=frag_local, frag_global=frag_global, frag_moment=frag_moment)


def normalize(tokens):
    floats = tokens.astype(jnp.float32)
    inverse_rms = lax.rsqrt(lax.optimization_barrier(jnp.mean(floats * floats, axis=-1, keepdims=True)) + 1e-05)
    return (floats * inverse_rms).astype(jnp.bfloat16)

def adam_direction(gradient, first_moment, second_moment, steps):
    first_new = 0.9 * first_moment + 0.1 * gradient
    second_new = 0.95 * second_moment + 0.05 * gradient * gradient
    first_fix = 1.0 - jnp.power(jnp.float32(0.9), steps)
    second_fix = 1.0 - jnp.power(jnp.float32(0.95), steps)
    return first_new / first_fix / (jnp.sqrt(second_new / second_fix) + 1e-08)

def outer_update(global_params, moment, local_mean):
    delta = global_params - local_mean
    moment_new = 0.9 * moment + delta
    return (global_params - 0.7 * (delta + 0.9 * moment_new), moment_new)

def reference(tokens_in, norm_gain, value_weight, value_cotangent, step_count, m_weight, v_weight, m_gain, v_gain, frag_local, frag_global, frag_moment):
    steps = step_count.astype(jnp.float32)

    def replica(operands):
        tokens, gain, weight, cotangent, first_w, second_w, first_g, second_g = operands
        normed = normalize(tokens)
        hidden = (normed.astype(jnp.float32) * gain.astype(jnp.float32)).astype(jnp.bfloat16)
        values = jnp.dot(hidden, weight, preferred_element_type=jnp.float32).astype(jnp.bfloat16)
        input_grad = jnp.dot(cotangent, weight.T, preferred_element_type=jnp.float32)
        weight_grad = jnp.dot(hidden.T, cotangent, preferred_element_type=jnp.float32) / TOKENS
        gain_grad = lax.optimization_barrier(jnp.sum(input_grad * normed.astype(jnp.float32), axis=0)) / TOKENS
        return (values, adam_direction(weight_grad, first_w, second_w, steps), adam_direction(gain_grad, first_g, second_g, steps))
    values, weight_step, gain_step = lax.map(replica, (tokens_in, norm_gain, value_weight, value_cotangent, m_weight, v_weight, m_gain, v_gain))
    summed = lax.optimization_barrier(jnp.sum(frag_local, axis=0))
    new_global, new_moment = outer_update(frag_global, frag_moment, summed / REPLICAS)
    return (values, weight_step, gain_step, new_global, new_moment)
```

```python
import jax
import jax.numpy as jnp
from jax import lax
from jax.sharding import Mesh
from jax.sharding import PartitionSpec as P

CORES = 2
SWAP = [(0, 1), (1, 0)]


def adam_direction(gradient, first_moment, second_moment, steps):
    first_new = 0.9 * first_moment + 0.1 * gradient
    second_new = 0.95 * second_moment + 0.05 * gradient * gradient
    first_fix = 1.0 - jnp.power(jnp.float32(0.9), steps)
    second_fix = 1.0 - jnp.power(jnp.float32(0.95), steps)
    return first_new / first_fix / (jnp.sqrt(second_new / second_fix) + 1e-08)


def outer_update(global_params, moment, local_mean):
    delta = global_params - local_mean
    moment_new = 0.9 * moment + delta
    return (global_params - 0.7 * (delta + 0.9 * moment_new), moment_new)


def exchange(blocks, axis):
    return lax.all_to_all(blocks, axis, 0, 0, tiled=True)


def spread(block, axis):
    return exchange(jnp.broadcast_to(block[None], (lax.axis_size(axis),) + block.shape), axis)


def local(
    tokens_in,
    norm_gain,
    value_weight,
    value_cotangent,
    step_count,
    m_weight,
    v_weight,
    m_gain,
    v_gain,
    frag_local,
    frag_global,
    frag_moment,
):
    tokens = tokens_in[0]
    gain = norm_gain[0].astype(jnp.float32)
    weight = value_weight[0].astype(jnp.float32)
    cotangent = value_cotangent[0].astype(jnp.float32)
    rows, width = tokens.shape
    head = weight.shape[1]
    chips = lax.axis_size("chip")
    token_total = rows * chips * CORES
    first_core = lax.axis_index("core") == 0

    scaled_weight = (weight * gain[:, None]).astype(jnp.bfloat16)
    own_weight = spread(scaled_weight, "chip")
    other_weight = lax.ppermute(own_weight, "core", SWAP)

    floats = tokens.astype(jnp.float32)
    inverse_rms = lax.rsqrt(jnp.mean(floats * floats, axis=-1, keepdims=True) + 1e-05)
    scaled_cotangent = (cotangent * inverse_rms).astype(jnp.bfloat16)
    parts = tokens.reshape(rows, chips, CORES, -1)
    own_tokens = jnp.where(first_core, parts[:, :, 0], parts[:, :, 1]).reshape(rows, -1)
    other_tokens = jnp.where(first_core, parts[:, :, 1], parts[:, :, 0]).reshape(rows, -1)

    def gradient_term(some_tokens):
        return lax.dot_general(
            some_tokens, scaled_cotangent, (((0,), (0,)), ((), ())), preferred_element_type=jnp.float32
        )

    arrived = lax.ppermute(gradient_term(other_tokens).astype(jnp.bfloat16), "core", SWAP)
    chip_term = (gradient_term(own_tokens) + arrived.astype(jnp.float32)).astype(jnp.bfloat16)
    terms = exchange(chip_term.reshape(chips, -1, head), "chip")
    gradient = jnp.sum(terms.astype(jnp.float32), axis=0) / token_total

    replicas = lax.axis_size("rep")
    frag = frag_local[0].astype(jnp.bfloat16)
    frag_terms = exchange(frag.reshape(replicas, -1, frag.shape[1]), "rep")
    frag_sum = jnp.sum(frag_terms.astype(jnp.float32), axis=0).astype(jnp.bfloat16)
    local_sum = spread(frag_sum, "rep").reshape(frag.shape).astype(jnp.float32)
    new_global, new_moment = outer_update(frag_global, frag_moment, local_sum / replicas)

    def product(some_tokens, some_weight):
        return jnp.dot(some_tokens, some_weight.reshape(-1, head), preferred_element_type=jnp.float32)

    summed = product(own_tokens, own_weight) + product(other_tokens, other_weight)
    values = (summed * inverse_rms).astype(jnp.bfloat16)

    steps = step_count.astype(jnp.float32)
    weight_step = adam_direction(gradient * gain[:, None], m_weight[0], v_weight[0], steps)
    gain_step = adam_direction(jnp.sum(weight * gradient, axis=1), m_gain[0], v_gain[0], steps)
    return (values[None], weight_step[None], gain_step[None], new_global, new_moment)


def solution(mesh):
    split = Mesh(mesh.devices.reshape(mesh.shape["rep"], -1, CORES), ("rep", "chip", "core"))
    fsdp = ("chip", "core")
    in_specs = (
        P("rep", fsdp, None),
        P("rep", fsdp),
        P("rep", fsdp, None),
        P("rep", fsdp, None),
        P(),
        P("rep", fsdp, None),
        P("rep", fsdp, None),
        P("rep", fsdp),
        P("rep", fsdp),
        P("rep", fsdp, None),
        P(fsdp, None),
        P(fsdp, None),
    )
    out_specs = (
        P("rep", fsdp, None),
        P("rep", fsdp, None),
        P("rep", fsdp),
        P(fsdp, None),
        P(fsdp, None),
    )
    return jax.shard_map(local, mesh=split, in_specs=in_specs, out_specs=out_specs, check_vma=False)
```

```python
import functools

import jax
import jax.numpy as jnp
from jax import lax
from jax.experimental import pallas as pl
from jax.experimental.pallas import tpu as pltpu
from jax.sharding import PartitionSpec as P

EIGHT = 8
FOUR = 4
LANES = 128


def chip_of(core, four, eight):
    if core:
        return eight * FOUR + four
    return (eight // FOUR * FOUR + four) * FOUR + eight % FOUR


def device_of(core, four, eight):
    return chip_of(core, four, eight) * 2 + core


EIGHT_GROUPS = [[device_of(core, four, eight) for eight in range(EIGHT)] for core in range(2) for four in range(FOUR)]
SWAP_CORES = [(device, device ^ 1) for device in range(2 * FOUR * EIGHT)]


def four_pairs(step):
    return [
        (device_of(core, four, eight), device_of(core, four ^ step, eight))
        for core in range(2)
        for four in range(FOUR)
        for eight in range(EIGHT)
    ]


def exchange(blocks, axis, groups=None):
    return lax.all_to_all(blocks, axis, 0, 0, axis_index_groups=groups, tiled=True)


def spread(block, count, axis, groups=None):
    return exchange(jnp.broadcast_to(block[None], (count,) + block.shape), axis, groups)


def call(kernel, *out_shapes):
    return pl.pallas_call(
        kernel,
        out_shape=out_shapes,
        compiler_params=pltpu.CompilerParams(vmem_limit_bytes=32 * 1024 * 1024),
    )


def lanes_of(block):
    return slice(block * LANES, (block + 1) * LANES)


def split_kernel(tokens_ref, cotangent_ref, keep_ref, send_ref, inverse_ref):
    device = lax.axis_index("fsdp")
    core = lax.rem(device, 2)
    chip = lax.div(device, 2)
    row, column = lax.div(chip, FOUR), lax.rem(chip, FOUR)
    fours = (lax.rem(row, FOUR), column)
    rows, width = tokens_ref.shape
    total = jnp.zeros((rows, LANES), jnp.float32)
    for block in range(width // LANES):
        floats = tokens_ref[:, lanes_of(block)].astype(jnp.float32)
        total += floats * floats
    inverse = lax.rsqrt(jnp.sum(total, axis=1, keepdims=True) / width + 1e-05)
    inverse_ref[...] = jnp.broadcast_to(inverse, (rows, LANES))
    send_ref[:, lanes_of(FOUR * EIGHT)] = (cotangent_ref[...].astype(jnp.float32) * inverse).astype(jnp.bfloat16)
    for step in range(FOUR):
        for eight in range(EIGHT):
            chips = [chip_of(kind, fours[kind] ^ step, eight) for kind in range(2)]
            for target, kind in ((keep_ref, core), (send_ref, 1 - core)):
                source = jnp.where(kind == 0, chips[0], chips[1]) * 2 + kind
                start = pl.multiple_of(source * LANES, LANES)
                target[:, lanes_of(step * EIGHT + eight)] = tokens_ref[:, pl.ds(start, LANES)]


def gradient_kernel(keep_ref, arrived_ref, send_ref, own_ref, *out_refs):
    last = lanes_of(FOUR * EIGHT)
    columns = EIGHT * LANES
    cotangents = jnp.concatenate([send_ref[:, last], arrived_ref[:, last]], axis=0)
    for step, out_ref in enumerate((own_ref,) + out_refs):
        part = slice(step * columns, (step + 1) * columns)
        both = jnp.concatenate([keep_ref[:, part], arrived_ref[:, part]], axis=0)
        term = lax.dot_general(cotangents, both, (((0,), (0,)), ((), ())), preferred_element_type=jnp.float32)
        out_ref[...] = term.astype(out_ref.dtype)


def add_kernel(own_ref, first_ref, second_ref, third_ref, out_ref):
    for block in range(EIGHT):
        part = lanes_of(block)
        total = own_ref[:, part]
        for ref in (first_ref, second_ref, third_ref):
            total += ref[:, part].astype(jnp.float32)
        out_ref[block] = total.astype(out_ref.dtype)


def values_kernel(keep_ref, arrived_ref, *refs):
    *weight_refs, own_ref, other_ref = refs
    columns = EIGHT * LANES
    total = jnp.zeros((2 * own_ref.shape[0], own_ref.shape[1]), jnp.float32)
    for step, weight_ref in enumerate(weight_refs):
        part = slice(step * columns, (step + 1) * columns)
        both = jnp.concatenate([keep_ref[:, part], arrived_ref[:, part]], axis=0)
        total += jnp.dot(both, weight_ref[...], preferred_element_type=jnp.float32)
    own_ref[...] = total[: own_ref.shape[0]]
    other_ref[...] = total[own_ref.shape[0] :]


def adam_direction(gradient, first_moment, second_moment, first_fix, second_fix):
    first_new = 0.9 * first_moment + 0.1 * gradient
    second_new = 0.95 * second_moment + 0.05 * gradient * gradient
    return first_new / first_fix / (jnp.sqrt(second_new / second_fix) + 1e-08)


def adam_kernel(
    token_total,
    terms_ref,
    weight_ref,
    gain_ref,
    fixes_ref,
    m_weight_ref,
    v_weight_ref,
    m_gain_ref,
    v_gain_ref,
    weight_step_ref,
    gain_step_ref,
):
    total = terms_ref[0].astype(jnp.float32)
    for block in range(1, EIGHT):
        total += terms_ref[block].astype(jnp.float32)
    gradient = total / token_total
    fixes = fixes_ref[0:1, :], fixes_ref[1:2, :]
    weight_gradient = (gradient * gain_ref[...].astype(jnp.float32)).T
    weight_step_ref[...] = adam_direction(weight_gradient, m_weight_ref[...], v_weight_ref[...], *fixes)
    gain_gradient = jnp.sum(gradient * weight_ref[...].astype(jnp.float32).T, axis=0, keepdims=True)
    gain_step_ref[...] = adam_direction(gain_gradient, m_gain_ref[...], v_gain_ref[...], *fixes)


def outer_update(global_params, moment, local_mean):
    delta = global_params - local_mean
    moment_new = 0.9 * moment + delta
    return (global_params - 0.7 * (delta + 0.9 * moment_new), moment_new)


def local(
    tokens_in,
    norm_gain,
    value_weight,
    value_cotangent,
    step_count,
    m_weight,
    v_weight,
    m_gain,
    v_gain,
    frag_local,
    frag_global,
    frag_moment,
):
    tokens = tokens_in[0]
    rows, width = tokens.shape
    head = value_weight.shape[2]
    half = width // 2
    columns = EIGHT * LANES
    token_total = rows * lax.axis_size("fsdp")

    gains = norm_gain[0].astype(jnp.float32)[:, None]
    scaled_weight = (value_weight[0].astype(jnp.float32) * gains).astype(jnp.bfloat16)
    weights = [spread(scaled_weight, EIGHT, "fsdp", EIGHT_GROUPS).reshape(columns, head)]
    weights += [lax.ppermute(weights[0], "fsdp", four_pairs(step)) for step in range(1, FOUR)]

    keep, send, inverse_rms = call(
        split_kernel,
        jax.ShapeDtypeStruct((rows, half), jnp.bfloat16),
        jax.ShapeDtypeStruct((rows, half + LANES), jnp.bfloat16),
        jax.ShapeDtypeStruct((rows, LANES), jnp.float32),
    )(tokens, value_cotangent[0])
    arrived = lax.ppermute(send, "fsdp", SWAP_CORES)

    own_term, *terms = call(
        gradient_kernel,
        jax.ShapeDtypeStruct((head, columns), jnp.float32),
        *[jax.ShapeDtypeStruct((head, columns), jnp.bfloat16)] * (FOUR - 1),
    )(keep, arrived, send)
    terms = [lax.ppermute(term, "fsdp", four_pairs(step)) for step, term in enumerate(terms, 1)]
    (summed,) = call(add_kernel, jax.ShapeDtypeStruct((EIGHT, head, LANES), jnp.bfloat16))(own_term, *terms)
    scattered = exchange(summed, "fsdp", EIGHT_GROUPS)
    steps = step_count.astype(jnp.float32)
    fixes = 1.0 - jnp.power(jnp.array([[0.9], [0.95]], jnp.float32), steps)
    weight_step, gain_step = call(
        functools.partial(adam_kernel, token_total),
        jax.ShapeDtypeStruct(m_weight.shape[1:], jnp.float32),
        jax.ShapeDtypeStruct(m_gain.shape, jnp.float32),
    )(
        scattered,
        value_weight[0],
        norm_gain,
        jnp.broadcast_to(fixes, (2, LANES)),
        m_weight[0],
        v_weight[0],
        m_gain,
        v_gain,
    )

    replicas = lax.axis_size("rep")
    frag = frag_local[0].astype(jnp.bfloat16)
    frag_terms = exchange(frag.reshape(replicas, -1, frag.shape[1]), "rep")
    frag_sum = jnp.sum(frag_terms.astype(jnp.float32), axis=0).astype(jnp.bfloat16)
    local_sum = spread(frag_sum, replicas, "rep").reshape(frag.shape).astype(jnp.float32)
    new_global, new_moment = outer_update(frag_global, frag_moment, local_sum / replicas)

    partial = jax.ShapeDtypeStruct((rows, head), jnp.float32)
    own_part, other_part = call(values_kernel, partial, partial)(keep, arrived, *weights)
    arrived_part = lax.ppermute(other_part, "fsdp", SWAP_CORES)
    values = ((own_part + arrived_part) * inverse_rms).astype(jnp.bfloat16)

    return (values[None], weight_step[None], gain_step, new_global, new_moment)


def solution(mesh):
    in_specs = (
        P("rep", "fsdp", None),
        P("rep", "fsdp"),
        P("rep", "fsdp", None),
        P("rep", "fsdp", None),
        P(),
        P("rep", "fsdp", None),
        P("rep", "fsdp", None),
        P("rep", "fsdp"),
        P("rep", "fsdp"),
        P("rep", "fsdp", None),
        P("fsdp", None),
        P("fsdp", None),
    )
    out_specs = (
        P("rep", "fsdp", None),
        P("rep", "fsdp", None),
        P("rep", "fsdp"),
        P("fsdp", None),
        P("fsdp", None),
    )
    return jax.shard_map(local, mesh=mesh, in_specs=in_specs, out_specs=out_specs, check_vma=False)
```

```python
import functools

import jax
import jax.numpy as jnp
from jax import lax
from jax.experimental import pallas as pl
from jax.experimental.pallas import tpu as pltpu
from jax.sharding import PartitionSpec as P

EIGHT = 8
FOUR = 4
LANES = 128


def chip_of(core, four, eight):
    if core:
        return eight * FOUR + four
    return (eight // FOUR * FOUR + four) * FOUR + eight % FOUR


def device_of(core, four, eight):
    return chip_of(core, four, eight) * 2 + core


EIGHT_GROUPS = [[device_of(core, four, eight) for eight in range(EIGHT)] for core in range(2) for four in range(FOUR)]
SWAP_CORES = [(device, device ^ 1) for device in range(2 * FOUR * EIGHT)]


def four_pairs(step):
    return [
        (device_of(core, four, eight), device_of(core, four ^ step, eight))
        for core in range(2)
        for four in range(FOUR)
        for eight in range(EIGHT)
    ]


def exchange(blocks, axis, groups=None):
    return lax.all_to_all(blocks, axis, 0, 0, axis_index_groups=groups, tiled=True)


def spread(block, count, axis, groups=None):
    return exchange(jnp.broadcast_to(block[None], (count,) + block.shape), axis, groups)


def call(kernel, *out_shapes, mebibytes=16, **specs):
    return pl.pallas_call(
        kernel,
        out_shape=out_shapes,
        **specs,
        compiler_params=pltpu.CompilerParams(vmem_limit_bytes=mebibytes * 1024 * 1024),
    )


def lanes_of(block):
    return slice(block * LANES, (block + 1) * LANES)


def split_kernel(
    tokens_hbm,
    cotangent_hbm,
    weight_hbm,
    gain_ref,
    keep_ref,
    send_ref,
    scaled_ref,
    inverse_ref,
    spread_ref,
    tokens_ref,
    cotangent_ref,
    weight_ref,
    semaphores,
):
    rows, width = tokens_ref.shape
    pieces = 4
    piece = width // pieces
    copies = [
        pltpu.make_async_copy(weight_hbm, weight_ref, semaphores.at[pieces]),
        pltpu.make_async_copy(cotangent_hbm, cotangent_ref, semaphores.at[pieces + 1]),
    ]
    for index in range(pieces):
        part = slice(index * piece, (index + 1) * piece)
        copies.append(pltpu.make_async_copy(tokens_hbm.at[:, part], tokens_ref.at[:, part], semaphores.at[index]))
    for copy in copies:
        copy.start()

    copies[0].wait()
    gains = jnp.broadcast_to(gain_ref[...].astype(jnp.float32), (LANES, LANES)).T
    scaled_weight = (weight_ref[...].astype(jnp.float32) * gains).astype(jnp.bfloat16)
    for eight in range(EIGHT):
        spread_ref[eight] = scaled_weight

    total = jnp.zeros((rows, LANES), jnp.float32)
    for index in range(pieces):
        copies[2 + index].wait()
        for block in range(index * piece // LANES, (index + 1) * piece // LANES):
            floats = tokens_ref[:, lanes_of(block)].astype(jnp.float32)
            total += floats * floats
    inverse = lax.rsqrt(jnp.sum(total, axis=1, keepdims=True) / width + 1e-05)
    inverse_ref[...] = jnp.broadcast_to(inverse, (rows, LANES))
    copies[1].wait()
    scaled = (cotangent_ref[...].astype(jnp.float32) * inverse).astype(jnp.bfloat16)
    scaled_ref[...] = scaled
    send_ref[:, lanes_of(FOUR * EIGHT)] = scaled

    device = lax.axis_index("fsdp")
    core = lax.rem(device, 2)
    chip = lax.div(device, 2)
    row, column = lax.div(chip, FOUR), lax.rem(chip, FOUR)
    fours = (lax.rem(row, FOUR), column)
    for step in range(FOUR):
        for eight in range(EIGHT):
            chips = [chip_of(kind, fours[kind] ^ step, eight) for kind in range(2)]
            for target, kind in ((keep_ref, core), (send_ref, 1 - core)):
                source = jnp.where(kind == 0, chips[0], chips[1]) * 2 + kind
                start = pl.multiple_of(source * LANES, LANES)
                target[:, lanes_of(step * EIGHT + eight)] = tokens_ref[:, pl.ds(start, LANES)]


def gradient_term(keep_ref, arrived_ref, scaled_ref, step):
    part = slice(step * EIGHT * LANES, (step + 1) * EIGHT * LANES)
    cotangents = jnp.concatenate([scaled_ref[...], arrived_ref[:, lanes_of(FOUR * EIGHT)]], axis=0)
    both = jnp.concatenate([keep_ref[:, part], arrived_ref[:, part]], axis=0)
    return lax.dot_general(cotangents, both, (((0,), (0,)), ((), ())), preferred_element_type=jnp.float32)


def outgoing_kernel(keep_ref, arrived_ref, scaled_ref, weight_ref, again_ref, *out_refs):
    again_ref[...] = scaled_ref[...]
    for step, out_ref in enumerate(out_refs, 1):
        term = gradient_term(keep_ref, arrived_ref, scaled_ref, step)
        for eight in range(EIGHT):
            out_ref[0, eight] = weight_ref[eight]
            out_ref[1, eight] = term[:, lanes_of(eight)].astype(jnp.bfloat16)


def add_kernel(keep_ref, arrived_ref, scaled_ref, first_ref, second_ref, third_ref, out_ref):
    own = gradient_term(keep_ref, arrived_ref, scaled_ref, 0)
    for eight in range(EIGHT):
        total = own[:, lanes_of(eight)]
        for ref in (first_ref, second_ref, third_ref):
            total += ref[1, eight].astype(jnp.float32)
        out_ref[eight] = total.astype(out_ref.dtype)


def values_kernel(keep_ref, arrived_ref, weight_ref, first_ref, second_ref, third_ref, own_ref, other_ref):
    columns = EIGHT * LANES
    rows, head = own_ref.shape
    total = jnp.zeros((2 * rows, head), jnp.float32)
    weights = [weight_ref[...]] + [ref[0] for ref in (first_ref, second_ref, third_ref)]
    for step, weight in enumerate(weights):
        part = slice(step * columns, (step + 1) * columns)
        both = jnp.concatenate([keep_ref[:, part], arrived_ref[:, part]], axis=0)
        total += jnp.dot(both, weight.reshape(columns, head), preferred_element_type=jnp.float32)
    own_ref[...] = total[:rows]
    other_ref[...] = total[rows:]


def adam_direction(gradient, first_moment, second_moment, first_fix, second_fix):
    first_new = 0.9 * first_moment + 0.1 * gradient
    second_new = 0.95 * second_moment + 0.05 * gradient * gradient
    return first_new / first_fix / (jnp.sqrt(second_new / second_fix) + 1e-08)


def adam_kernel(
    token_total,
    terms_ref,
    weight_ref,
    gain_ref,
    fixes_ref,
    m_weight_ref,
    v_weight_ref,
    m_gain_ref,
    v_gain_ref,
    weight_step_ref,
    gain_step_ref,
):
    total = terms_ref[0].astype(jnp.float32)
    for block in range(1, EIGHT):
        total += terms_ref[block].astype(jnp.float32)
    gradient = total / token_total
    fixes = fixes_ref[0:1, :], fixes_ref[1:2, :]
    weight_gradient = (gradient * gain_ref[...].astype(jnp.float32)).T
    weight_step_ref[...] = adam_direction(weight_gradient, m_weight_ref[...], v_weight_ref[...], *fixes)
    gain_gradient = jnp.sum(gradient * weight_ref[...].astype(jnp.float32).T, axis=0, keepdims=True)
    gain_step_ref[...] = adam_direction(gain_gradient, m_gain_ref[...], v_gain_ref[...], *fixes)


def outer_update(global_params, moment, local_mean):
    delta = global_params - local_mean
    moment_new = 0.9 * moment + delta
    return (global_params - 0.7 * (delta + 0.9 * moment_new), moment_new)


def local(
    tokens_in,
    norm_gain,
    value_weight,
    value_cotangent,
    step_count,
    m_weight,
    v_weight,
    m_gain,
    v_gain,
    frag_local,
    frag_global,
    frag_moment,
):
    rows, width = tokens_in.shape[1:]
    head = value_weight.shape[2]
    half = width // 2
    token_total = rows * lax.axis_size("fsdp")
    replicas = lax.axis_size("rep")
    frag_shape = frag_local.shape[1:]

    hbm = pl.BlockSpec(memory_space=pltpu.HBM)
    keep, send, scaled, inverse_rms, spread_weight = call(
        split_kernel,
        jax.ShapeDtypeStruct((rows, half), jnp.bfloat16),
        jax.ShapeDtypeStruct((rows, half + LANES), jnp.bfloat16),
        jax.ShapeDtypeStruct((rows, head), jnp.bfloat16),
        jax.ShapeDtypeStruct((rows, LANES), jnp.float32),
        jax.ShapeDtypeStruct((EIGHT, LANES, head), jnp.bfloat16),
        mebibytes=60,
        in_specs=[hbm, hbm, hbm, pl.BlockSpec(memory_space=pltpu.VMEM)],
        scratch_shapes=[
            pltpu.VMEM((rows, width), jnp.bfloat16),
            pltpu.VMEM((rows, head), jnp.bfloat16),
            pltpu.VMEM((LANES, head), jnp.bfloat16),
            pltpu.SemaphoreType.DMA((6,)),
        ],
    )(tokens_in[0], value_cotangent[0], value_weight[0], norm_gain)
    arrived = lax.ppermute(send, "fsdp", SWAP_CORES)
    weight = exchange(spread_weight, "fsdp", EIGHT_GROUPS)

    scaled, *outgoing = call(
        outgoing_kernel,
        jax.ShapeDtypeStruct(scaled.shape, scaled.dtype),
        *[jax.ShapeDtypeStruct((2, EIGHT, head, LANES), jnp.bfloat16)] * (FOUR - 1),
    )(keep, arrived, scaled, weight)
    frag = frag_local[0].astype(jnp.bfloat16).reshape(replicas, -1, frag_shape[1])
    scaled, frag = lax.optimization_barrier((scaled, frag))
    incoming = [lax.ppermute(blocks, "fsdp", four_pairs(step)) for step, blocks in enumerate(outgoing, 1)]
    frag_terms = exchange(frag, "rep")
    frag_sum = jnp.sum(frag_terms.astype(jnp.float32), axis=0).astype(jnp.bfloat16)
    scaled, frag_sum = lax.optimization_barrier((scaled, frag_sum))
    local_sum = spread(frag_sum, replicas, "rep")

    (summed,) = call(add_kernel, jax.ShapeDtypeStruct((EIGHT, head, LANES), jnp.bfloat16))(
        keep, arrived, scaled, *incoming
    )
    summed, local_sum = lax.optimization_barrier((summed, local_sum))
    scattered = exchange(summed, "fsdp", EIGHT_GROUPS)
    local_mean = local_sum.reshape(frag_shape).astype(jnp.float32) / replicas
    new_global, new_moment = outer_update(frag_global, frag_moment, local_mean)

    partial = jax.ShapeDtypeStruct((rows, head), jnp.float32)
    own_part, other_part = call(values_kernel, partial, partial)(keep, arrived, weight, *incoming)
    arrived_part = lax.ppermute(other_part, "fsdp", SWAP_CORES)
    values = ((own_part + arrived_part) * inverse_rms).astype(jnp.bfloat16)

    steps = step_count.astype(jnp.float32)
    fixes = 1.0 - jnp.power(jnp.array([[0.9], [0.95]], jnp.float32), steps)
    weight_step, gain_step = call(
        functools.partial(adam_kernel, token_total),
        jax.ShapeDtypeStruct(m_weight.shape[1:], jnp.float32),
        jax.ShapeDtypeStruct(m_gain.shape, jnp.float32),
    )(
        scattered,
        value_weight[0],
        norm_gain,
        jnp.broadcast_to(fixes, (2, LANES)),
        m_weight[0],
        v_weight[0],
        m_gain,
        v_gain,
    )
    return (values[None], weight_step[None], gain_step, new_global, new_moment)


def solution(mesh):
    in_specs = (
        P("rep", "fsdp", None),
        P("rep", "fsdp"),
        P("rep", "fsdp", None),
        P("rep", "fsdp", None),
        P(),
        P("rep", "fsdp", None),
        P("rep", "fsdp", None),
        P("rep", "fsdp"),
        P("rep", "fsdp"),
        P("rep", "fsdp", None),
        P("fsdp", None),
        P("fsdp", None),
    )
    out_specs = (
        P("rep", "fsdp", None),
        P("rep", "fsdp", None),
        P("rep", "fsdp"),
        P("fsdp", None),
        P("fsdp", None),
    )
    return jax.shard_map(local, mesh=mesh, in_specs=in_specs, out_specs=out_specs, check_vma=False)
```

```python
import functools

import jax
import jax.numpy as jnp
from jax import lax
from jax.experimental import pallas as pl
from jax.experimental.pallas import tpu as pltpu
from jax.sharding import PartitionSpec as P

EIGHT = 8
FOUR = 4
LANES = 128


def chip_of(core, four, eight):
    if core:
        return eight * FOUR + four
    return (eight // FOUR * FOUR + four) * FOUR + eight % FOUR


def device_of(core, four, eight):
    return chip_of(core, four, eight) * 2 + core


SIXTEEN_GROUPS = [
    [device_of(core, 2 * high + low, eight) for high in range(2) for eight in range(EIGHT)]
    for core in range(2)
    for low in range(2)
]
EIGHT_GROUPS = [[device_of(core, four, eight) for eight in range(EIGHT)] for core in range(2) for four in range(FOUR)]
SWAP_CORES = [(device, device ^ 1) for device in range(2 * FOUR * EIGHT)]


def four_pairs(step):
    return [
        (device_of(core, four, eight), device_of(core, four ^ step, eight))
        for core in range(2)
        for four in range(FOUR)
        for eight in range(EIGHT)
    ]


def exchange(blocks, axis, groups=None):
    return lax.all_to_all(blocks, axis, 0, 0, axis_index_groups=groups, tiled=True)


def spread(block, count, axis, groups=None):
    return exchange(jnp.broadcast_to(block[None], (count,) + block.shape), axis, groups)


def call(kernel, *out_shapes, mebibytes=16, **specs):
    return pl.pallas_call(
        kernel,
        out_shape=out_shapes,
        **specs,
        compiler_params=pltpu.CompilerParams(vmem_limit_bytes=mebibytes * 1024 * 1024),
    )


def place():
    device = lax.axis_index("fsdp")
    chip = lax.div(device, 2)
    row, column = lax.div(chip, FOUR), lax.rem(chip, FOUR)
    return lax.rem(device, 2), (lax.rem(row, FOUR), column)


def lanes_of(block):
    return slice(block * LANES, (block + 1) * LANES)


def split_kernel(
    tokens_hbm,
    cotangent_hbm,
    weight_hbm,
    gain_ref,
    keep_ref,
    send_ref,
    scaled_ref,
    inverse_ref,
    spread_ref,
    tokens_ref,
    cotangent_ref,
    weight_ref,
    semaphores,
):
    rows, width = tokens_ref.shape
    pieces = 4
    piece = width // pieces
    copies = [
        pltpu.make_async_copy(weight_hbm, weight_ref, semaphores.at[pieces]),
        pltpu.make_async_copy(cotangent_hbm, cotangent_ref, semaphores.at[pieces + 1]),
    ]
    for index in range(pieces):
        part = slice(index * piece, (index + 1) * piece)
        copies.append(pltpu.make_async_copy(tokens_hbm.at[:, part], tokens_ref.at[:, part], semaphores.at[index]))
    for copy in copies:
        copy.start()

    copies[0].wait()
    gains = jnp.broadcast_to(gain_ref[...].astype(jnp.float32), (LANES, LANES)).T
    scaled_weight = (weight_ref[...].astype(jnp.float32) * gains).astype(jnp.bfloat16)
    for block in range(spread_ref.shape[0]):
        spread_ref[block] = scaled_weight

    total = jnp.zeros((rows, LANES), jnp.float32)
    for index in range(pieces):
        copies[2 + index].wait()
        for block in range(index * piece // LANES, (index + 1) * piece // LANES):
            floats = tokens_ref[:, lanes_of(block)].astype(jnp.float32)
            total += floats * floats
    inverse = lax.rsqrt(jnp.sum(total, axis=1, keepdims=True) / width + 1e-05)
    inverse_ref[...] = jnp.broadcast_to(inverse, (rows, LANES))
    copies[1].wait()
    scaled = (cotangent_ref[...].astype(jnp.float32) * inverse).astype(jnp.bfloat16)
    scaled_ref[...] = scaled
    send_ref[:, lanes_of(FOUR * EIGHT)] = scaled

    core, fours = place()
    for step in range(FOUR):
        for eight in range(EIGHT):
            chips = [chip_of(kind, fours[kind] ^ step, eight) for kind in range(2)]
            for target, kind in ((keep_ref, core), (send_ref, 1 - core)):
                source = jnp.where(kind == 0, chips[0], chips[1]) * 2 + kind
                start = pl.multiple_of(source * LANES, LANES)
                target[:, lanes_of(step * EIGHT + eight)] = tokens_ref[:, pl.ds(start, LANES)]


def gradient_term(keep_ref, arrived_ref, scaled_ref, step):
    part = slice(step * EIGHT * LANES, (step + 1) * EIGHT * LANES)
    cotangents = jnp.concatenate([scaled_ref[...], arrived_ref[:, lanes_of(FOUR * EIGHT)]], axis=0)
    both = jnp.concatenate([keep_ref[:, part], arrived_ref[:, part]], axis=0)
    return lax.dot_general(cotangents, both, (((0,), (0,)), ((), ())), preferred_element_type=jnp.float32)


def outgoing_kernel(keep_ref, arrived_ref, scaled_ref, again_ref, *out_refs):
    again_ref[...] = scaled_ref[...]
    for step, out_ref in enumerate(out_refs, 1):
        term = gradient_term(keep_ref, arrived_ref, scaled_ref, step)
        for eight in range(EIGHT):
            out_ref[eight] = term[:, lanes_of(eight)].astype(jnp.bfloat16)


def add_kernel(keep_ref, arrived_ref, scaled_ref, first_ref, second_ref, third_ref, out_ref):
    own = gradient_term(keep_ref, arrived_ref, scaled_ref, 0)
    for eight in range(EIGHT):
        total = own[:, lanes_of(eight)]
        for ref in (first_ref, second_ref, third_ref):
            total += ref[eight].astype(jnp.float32)
        out_ref[eight] = total.astype(out_ref.dtype)


def values_kernel(keep_ref, arrived_ref, own_weight_ref, partner_weight_ref, own_ref, other_ref):
    core, fours = place()
    high = jnp.where(core == 0, fours[0], fours[1]) // 2
    columns = EIGHT * LANES
    rows, head = own_ref.shape
    total = jnp.zeros((2 * rows, head), jnp.float32)
    for step in range(FOUR):
        part = slice(step * columns, (step + 1) * columns)
        both = jnp.concatenate([keep_ref[:, part], arrived_ref[:, part]], axis=0)
        blocks = pl.ds((high ^ (step // 2)) * EIGHT, EIGHT)
        weight = (partner_weight_ref if step % 2 else own_weight_ref)[blocks].reshape(columns, head)
        total += jnp.dot(both, weight, preferred_element_type=jnp.float32)
    own_ref[...] = total[:rows]
    other_ref[...] = total[rows:]


def adam_direction(gradient, first_moment, second_moment, first_fix, second_fix):
    first_new = 0.9 * first_moment + 0.1 * gradient
    second_new = 0.95 * second_moment + 0.05 * gradient * gradient
    return first_new / first_fix / (jnp.sqrt(second_new / second_fix) + 1e-08)


def adam_kernel(
    token_total,
    terms_ref,
    weight_ref,
    gain_ref,
    fixes_ref,
    m_weight_ref,
    v_weight_ref,
    m_gain_ref,
    v_gain_ref,
    weight_step_ref,
    gain_step_ref,
):
    total = terms_ref[0].astype(jnp.float32)
    for block in range(1, EIGHT):
        total += terms_ref[block].astype(jnp.float32)
    gradient = total / token_total
    fixes = fixes_ref[0:1, :], fixes_ref[1:2, :]
    weight_gradient = (gradient * gain_ref[...].astype(jnp.float32)).T
    weight_step_ref[...] = adam_direction(weight_gradient, m_weight_ref[...], v_weight_ref[...], *fixes)
    gain_gradient = jnp.sum(gradient * weight_ref[...].astype(jnp.float32).T, axis=0, keepdims=True)
    gain_step_ref[...] = adam_direction(gain_gradient, m_gain_ref[...], v_gain_ref[...], *fixes)


def outer_update(global_params, moment, local_mean):
    delta = global_params - local_mean
    moment_new = 0.9 * moment + delta
    return (global_params - 0.7 * (delta + 0.9 * moment_new), moment_new)


def local(
    tokens_in,
    norm_gain,
    value_weight,
    value_cotangent,
    step_count,
    m_weight,
    v_weight,
    m_gain,
    v_gain,
    frag_local,
    frag_global,
    frag_moment,
):
    rows, width = tokens_in.shape[1:]
    head = value_weight.shape[2]
    half = width // 2
    token_total = rows * lax.axis_size("fsdp")
    replicas = lax.axis_size("rep")
    frag_shape = frag_local.shape[1:]

    hbm = pl.BlockSpec(memory_space=pltpu.HBM)
    keep, send, scaled, inverse_rms, spread_weight = call(
        split_kernel,
        jax.ShapeDtypeStruct((rows, half), jnp.bfloat16),
        jax.ShapeDtypeStruct((rows, half + LANES), jnp.bfloat16),
        jax.ShapeDtypeStruct((rows, head), jnp.bfloat16),
        jax.ShapeDtypeStruct((rows, LANES), jnp.float32),
        jax.ShapeDtypeStruct((2 * EIGHT, LANES, head), jnp.bfloat16),
        mebibytes=60,
        in_specs=[hbm, hbm, hbm, pl.BlockSpec(memory_space=pltpu.VMEM)],
        scratch_shapes=[
            pltpu.VMEM((rows, width), jnp.bfloat16),
            pltpu.VMEM((rows, head), jnp.bfloat16),
            pltpu.VMEM((LANES, head), jnp.bfloat16),
            pltpu.SemaphoreType.DMA((6,)),
        ],
    )(tokens_in[0], value_cotangent[0], value_weight[0], norm_gain)
    arrived = lax.ppermute(send, "fsdp", SWAP_CORES)
    weight = exchange(spread_weight, "fsdp", SIXTEEN_GROUPS)

    scaled, *outgoing = call(
        outgoing_kernel,
        jax.ShapeDtypeStruct(scaled.shape, scaled.dtype),
        *[jax.ShapeDtypeStruct((EIGHT, head, LANES), jnp.bfloat16)] * (FOUR - 1),
    )(keep, arrived, scaled)
    incoming = [lax.ppermute(blocks, "fsdp", four_pairs(step)) for step, blocks in enumerate(outgoing, 1)]
    frag = frag_local[0].astype(jnp.bfloat16).reshape(replicas, -1, frag_shape[1])
    *incoming, frag = lax.optimization_barrier((*incoming, frag))
    partner_weight = lax.ppermute(weight, "fsdp", four_pairs(1))
    frag_terms = exchange(frag, "rep")
    frag_sum = jnp.sum(frag_terms.astype(jnp.float32), axis=0).astype(jnp.bfloat16)
    local_sum = spread(frag_sum, replicas, "rep")

    (summed,) = call(add_kernel, jax.ShapeDtypeStruct((EIGHT, head, LANES), jnp.bfloat16))(
        keep, arrived, scaled, *incoming
    )
    summed, keep, arrived = lax.optimization_barrier((summed, keep, arrived))
    scattered = exchange(summed, "fsdp", EIGHT_GROUPS)
    local_mean = local_sum.reshape(frag_shape).astype(jnp.float32) / replicas
    new_global, new_moment = outer_update(frag_global, frag_moment, local_mean)

    partial = jax.ShapeDtypeStruct((rows, head), jnp.float32)
    own_part, other_part = call(values_kernel, partial, partial)(keep, arrived, weight, partner_weight)
    arrived_part = lax.ppermute(other_part, "fsdp", SWAP_CORES)
    values = ((own_part + arrived_part) * inverse_rms).astype(jnp.bfloat16)

    steps = step_count.astype(jnp.float32)
    fixes = 1.0 - jnp.power(jnp.array([[0.9], [0.95]], jnp.float32), steps)
    weight_step, gain_step = call(
        functools.partial(adam_kernel, token_total),
        jax.ShapeDtypeStruct(m_weight.shape[1:], jnp.float32),
        jax.ShapeDtypeStruct(m_gain.shape, jnp.float32),
    )(
        scattered,
        value_weight[0],
        norm_gain,
        jnp.broadcast_to(fixes, (2, LANES)),
        m_weight[0],
        v_weight[0],
        m_gain,
        v_gain,
    )
    return (values[None], weight_step[None], gain_step, new_global, new_moment)


def solution(mesh):
    in_specs = (
        P("rep", "fsdp", None),
        P("rep", "fsdp"),
        P("rep", "fsdp", None),
        P("rep", "fsdp", None),
        P(),
        P("rep", "fsdp", None),
        P("rep", "fsdp", None),
        P("rep", "fsdp"),
        P("rep", "fsdp"),
        P("rep", "fsdp", None),
        P("fsdp", None),
        P("fsdp", None),
    )
    out_specs = (
        P("rep", "fsdp", None),
        P("rep", "fsdp", None),
        P("rep", "fsdp"),
        P("fsdp", None),
        P("fsdp", None),
    )
    return jax.shard_map(local, mesh=mesh, in_specs=in_specs, out_specs=out_specs, check_vma=False)
```

```python
import functools

import jax
import jax.numpy as jnp
from jax import lax
from jax.experimental import pallas as pl
from jax.experimental.pallas import tpu as pltpu
from jax.sharding import PartitionSpec as P

EIGHT = 8
FOUR = 4
LANES = 128


def chip_of(core, four, eight):
    row = (2 * (eight // 2) + (four >> 1) + core) & 7
    column = (2 * (eight % 2) + (four & 1) + core) & 3
    return row * 4 + column


def device_of(core, four, eight):
    return chip_of(core, four, eight) * 2 + core


EIGHT_GROUPS = [[device_of(core, four, eight) for eight in range(EIGHT)] for core in range(2) for four in range(FOUR)]
SWAP_CORES = [(device, device ^ 1) for device in range(2 * FOUR * EIGHT)]


def four_pairs(step):
    return [
        (device_of(core, four, eight), device_of(core, four ^ step, eight))
        for core in range(2)
        for four in range(FOUR)
        for eight in range(EIGHT)
    ]


def exchange(blocks, axis, groups=None):
    return lax.all_to_all(blocks, axis, 0, 0, axis_index_groups=groups, tiled=True)


def spread(block, count, axis, groups=None):
    return exchange(jnp.broadcast_to(block[None], (count,) + block.shape), axis, groups)


def call(kernel, *out_shapes, mebibytes=16, **specs):
    return pl.pallas_call(
        kernel,
        out_shape=out_shapes,
        **specs,
        compiler_params=pltpu.CompilerParams(vmem_limit_bytes=mebibytes * 1024 * 1024),
    )


def part_of(index, head):
    return pl.BlockSpec((1, EIGHT, head, LANES), lambda i: (index, 0, 0, 0))


def lanes_of(block):
    return slice(block * LANES, (block + 1) * LANES)


def split_kernel(
    tokens_hbm,
    cotangent_hbm,
    weight_hbm,
    gain_ref,
    keep_hbm,
    send_hbm,
    scaled_ref,
    inverse_ref,
    spread_ref,
    tokens_ref,
    cotangent_ref,
    weight_ref,
    keep_ref,
    send_ref,
    in_semaphores,
    out_semaphores,
):
    rows, width = tokens_ref.shape
    pieces = 4
    piece = width // pieces
    copies = [
        pltpu.make_async_copy(weight_hbm, weight_ref, in_semaphores.at[pieces]),
        pltpu.make_async_copy(cotangent_hbm, cotangent_ref, in_semaphores.at[pieces + 1]),
    ]
    for index in range(pieces):
        part = slice(index * piece, (index + 1) * piece)
        copies.append(pltpu.make_async_copy(tokens_hbm.at[:, part], tokens_ref.at[:, part], in_semaphores.at[index]))
    for copy in copies:
        copy.start()

    copies[0].wait()
    gains = jnp.broadcast_to(gain_ref[...].astype(jnp.float32), (LANES, LANES)).T
    scaled_weight = (weight_ref[...].astype(jnp.float32) * gains).astype(jnp.bfloat16)
    for eight in range(EIGHT):
        spread_ref[eight] = scaled_weight

    def squares(index):
        total = jnp.zeros((rows, LANES), jnp.float32)
        for block in range(index * piece // LANES, (index + 1) * piece // LANES):
            floats = tokens_ref[:, lanes_of(block)].astype(jnp.float32)
            total += floats * floats
        return total

    total = jnp.zeros((rows, LANES), jnp.float32)
    for index in range(pieces - 1):
        copies[2 + index].wait()
        total += squares(index)
    copies[1 + pieces].wait()

    device = lax.axis_index("fsdp")
    core, row, column = device & 1, device >> 3, (device >> 1) & 3
    out_copies = []
    for step in range(FOUR):
        part = slice(step * EIGHT * LANES, (step + 1) * EIGHT * LANES)
        for target, target_hbm, kind in ((keep_ref, keep_hbm, core), (send_ref, send_hbm, 1 - core)):
            four = (((row + kind) & 1) * 2 + ((column + kind) & 1)) ^ step
            for eight in range(EIGHT):
                start = pl.multiple_of(device_of(kind, four, eight) * LANES, LANES)
                target[:, lanes_of(step * EIGHT + eight)] = tokens_ref[:, pl.ds(start, LANES)]
            semaphore = out_semaphores.at[len(out_copies)]
            out_copies.append(pltpu.make_async_copy(target.at[:, part], target_hbm.at[:, part], semaphore))
            out_copies[-1].start()

    total += squares(pieces - 1)
    inverse = lax.rsqrt(jnp.sum(total, axis=1, keepdims=True) / width + 1e-05)
    inverse_ref[...] = jnp.broadcast_to(inverse, (rows, LANES))
    copies[1].wait()
    scaled = (cotangent_ref[...].astype(jnp.float32) * inverse).astype(jnp.bfloat16)
    scaled_ref[...] = scaled
    last = lanes_of(FOUR * EIGHT)
    send_ref[:, last] = scaled
    out_copies.append(
        pltpu.make_async_copy(send_ref.at[:, last], send_hbm.at[:, last], out_semaphores.at[len(out_copies)])
    )
    out_copies[-1].start()
    for copy in out_copies:
        copy.wait()


def gradient_term(keep_ref, arrived_ref, scaled_ref, step):
    part = slice(step * EIGHT * LANES, (step + 1) * EIGHT * LANES)
    cotangents = jnp.concatenate([scaled_ref[...], arrived_ref[:, lanes_of(FOUR * EIGHT)]], axis=0)
    both = jnp.concatenate([keep_ref[:, part], arrived_ref[:, part]], axis=0)
    return lax.dot_general(cotangents, both, (((0,), (0,)), ((), ())), preferred_element_type=jnp.float32)


def outgoing_kernel(keep_ref, arrived_ref, scaled_ref, weight_ref, again_ref, *out_refs):
    again_ref[...] = scaled_ref[...]
    for step, out_ref in enumerate(out_refs, 1):
        term = gradient_term(keep_ref, arrived_ref, scaled_ref, step)
        for eight in range(EIGHT):
            out_ref[0, eight] = weight_ref[eight]
            out_ref[1, eight] = term[:, lanes_of(eight)].astype(jnp.bfloat16)


def add_kernel(keep_ref, arrived_ref, scaled_ref, first_ref, second_ref, third_ref, out_ref):
    own = gradient_term(keep_ref, arrived_ref, scaled_ref, 0)
    for eight in range(EIGHT):
        total = own[:, lanes_of(eight)]
        for ref in (first_ref, second_ref, third_ref):
            total += ref[0, eight].astype(jnp.float32)
        out_ref[eight] = total.astype(out_ref.dtype)


def values_kernel(keep_ref, arrived_ref, weight_ref, first_ref, second_ref, third_ref, own_ref, other_ref):
    columns = EIGHT * LANES
    rows, head = own_ref.shape
    total = jnp.zeros((2 * rows, head), jnp.float32)
    weights = [weight_ref[...]] + [ref[0] for ref in (first_ref, second_ref, third_ref)]
    for step, weight in enumerate(weights):
        part = slice(step * columns, (step + 1) * columns)
        both = jnp.concatenate([keep_ref[:, part], arrived_ref[:, part]], axis=0)
        total += jnp.dot(both, weight.reshape(columns, head), preferred_element_type=jnp.float32)
    own_ref[...] = total[:rows]
    other_ref[...] = total[rows:]


def adam_direction(gradient, first_moment, second_moment, first_fix, second_fix):
    first_new = 0.9 * first_moment + 0.1 * gradient
    second_new = 0.95 * second_moment + 0.05 * gradient * gradient
    return first_new / first_fix / (jnp.sqrt(second_new / second_fix) + 1e-08)


def adam_kernel(
    token_total,
    terms_ref,
    weight_ref,
    gain_ref,
    fixes_ref,
    m_weight_ref,
    v_weight_ref,
    m_gain_ref,
    v_gain_ref,
    weight_step_ref,
    gain_step_ref,
):
    total = terms_ref[0].astype(jnp.float32)
    for block in range(1, EIGHT):
        total += terms_ref[block].astype(jnp.float32)
    gradient = total / token_total
    fixes = fixes_ref[0:1, :], fixes_ref[1:2, :]
    weight_gradient = (gradient * gain_ref[...].astype(jnp.float32)).T
    weight_step_ref[...] = adam_direction(weight_gradient, m_weight_ref[...], v_weight_ref[...], *fixes)
    gain_gradient = jnp.sum(gradient * weight_ref[...].astype(jnp.float32).T, axis=0, keepdims=True)
    gain_step_ref[...] = adam_direction(gain_gradient, m_gain_ref[...], v_gain_ref[...], *fixes)


def outer_update(global_params, moment, local_mean):
    delta = global_params - local_mean
    moment_new = 0.9 * moment + delta
    return (global_params - 0.7 * (delta + 0.9 * moment_new), moment_new)


def local(
    tokens_in,
    norm_gain,
    value_weight,
    value_cotangent,
    step_count,
    m_weight,
    v_weight,
    m_gain,
    v_gain,
    frag_local,
    frag_global,
    frag_moment,
):
    rows, width = tokens_in.shape[1:]
    head = value_weight.shape[2]
    half = width // 2
    token_total = rows * lax.axis_size("fsdp")
    replicas = lax.axis_size("rep")
    frag_shape = frag_local.shape[1:]

    hbm = pl.BlockSpec(memory_space=pltpu.HBM)
    keep, send, scaled, inverse_rms, spread_weight = call(
        split_kernel,
        jax.ShapeDtypeStruct((rows, half), jnp.bfloat16),
        jax.ShapeDtypeStruct((rows, half + LANES), jnp.bfloat16),
        jax.ShapeDtypeStruct((rows, head), jnp.bfloat16),
        jax.ShapeDtypeStruct((rows, LANES), jnp.float32),
        jax.ShapeDtypeStruct((EIGHT, LANES, head), jnp.bfloat16),
        mebibytes=60,
        in_specs=[hbm, hbm, hbm, pl.BlockSpec(memory_space=pltpu.VMEM)],
        out_specs=[hbm, hbm] + [pl.BlockSpec(memory_space=pltpu.VMEM)] * 3,
        scratch_shapes=[
            pltpu.VMEM((rows, width), jnp.bfloat16),
            pltpu.VMEM((rows, head), jnp.bfloat16),
            pltpu.VMEM((LANES, head), jnp.bfloat16),
            pltpu.VMEM((rows, half), jnp.bfloat16),
            pltpu.VMEM((rows, half + LANES), jnp.bfloat16),
            pltpu.SemaphoreType.DMA((6,)),
            pltpu.SemaphoreType.DMA((2 * FOUR + 1,)),
        ],
    )(tokens_in[0], value_cotangent[0], value_weight[0], norm_gain)
    arrived = lax.ppermute(send, "fsdp", SWAP_CORES)
    weight = exchange(spread_weight, "fsdp", EIGHT_GROUPS)

    scaled, *outgoing = call(
        outgoing_kernel,
        jax.ShapeDtypeStruct(scaled.shape, scaled.dtype),
        *[jax.ShapeDtypeStruct((2, EIGHT, head, LANES), jnp.bfloat16)] * (FOUR - 1),
    )(keep, arrived, scaled, weight)
    frag = frag_local[0].astype(jnp.bfloat16).reshape(replicas, -1, frag_shape[1])
    scaled, frag = lax.optimization_barrier((scaled, frag))
    incoming = [lax.ppermute(blocks, "fsdp", four_pairs(step)) for step, blocks in enumerate(outgoing, 1)]
    frag_terms = exchange(frag, "rep")
    frag_sum = jnp.sum(frag_terms.astype(jnp.float32), axis=0).astype(jnp.bfloat16)
    scaled, frag_sum = lax.optimization_barrier((scaled, frag_sum))
    local_sum = spread(frag_sum, replicas, "rep")

    whole = pl.BlockSpec(memory_space=pltpu.VMEM)
    (summed,) = call(
        add_kernel,
        jax.ShapeDtypeStruct((EIGHT, head, LANES), jnp.bfloat16),
        grid=(1,),
        in_specs=[whole] * 3 + [part_of(1, head)] * (FOUR - 1),
    )(keep, arrived, scaled, *incoming)
    summed, local_sum = lax.optimization_barrier((summed, local_sum))
    scattered = exchange(summed, "fsdp", EIGHT_GROUPS)
    local_mean = local_sum.reshape(frag_shape).astype(jnp.float32) / replicas
    new_global, new_moment = outer_update(frag_global, frag_moment, local_mean)

    partial = jax.ShapeDtypeStruct((rows, head), jnp.float32)
    own_part, other_part = call(
        values_kernel, partial, partial, grid=(1,), in_specs=[whole] * 3 + [part_of(0, head)] * (FOUR - 1)
    )(keep, arrived, weight, *incoming)
    arrived_part = lax.ppermute(other_part, "fsdp", SWAP_CORES)
    values = ((own_part + arrived_part) * inverse_rms).astype(jnp.bfloat16)

    steps = step_count.astype(jnp.float32)
    fixes = 1.0 - jnp.power(jnp.array([[0.9], [0.95]], jnp.float32), steps)
    weight_step, gain_step = call(
        functools.partial(adam_kernel, token_total),
        jax.ShapeDtypeStruct(m_weight.shape[1:], jnp.float32),
        jax.ShapeDtypeStruct(m_gain.shape, jnp.float32),
    )(
        scattered,
        value_weight[0],
        norm_gain,
        jnp.broadcast_to(fixes, (2, LANES)),
        m_weight[0],
        v_weight[0],
        m_gain,
        v_gain,
    )
    return (values[None], weight_step[None], gain_step, new_global, new_moment)


def solution(mesh):
    in_specs = (
        P("rep", "fsdp", None),
        P("rep", "fsdp"),
        P("rep", "fsdp", None),
        P("rep", "fsdp", None),
        P(),
        P("rep", "fsdp", None),
        P("rep", "fsdp", None),
        P("rep", "fsdp"),
        P("rep", "fsdp"),
        P("rep", "fsdp", None),
        P("fsdp", None),
        P("fsdp", None),
    )
    out_specs = (
        P("rep", "fsdp", None),
        P("rep", "fsdp", None),
        P("rep", "fsdp"),
        P("fsdp", None),
        P("fsdp", None),
    )
    return jax.shard_map(local, mesh=mesh, in_specs=in_specs, out_specs=out_specs, check_vma=False)
```

```python
import functools

import jax
import jax.numpy as jnp
from jax import lax
from jax.experimental import pallas as pl
from jax.experimental.pallas import tpu as pltpu
from jax.sharding import PartitionSpec as P

EIGHT = 8
FOUR = 4
ALONG_X, ALONG_Y = 1, 2
LANES = 128


def chip_of(core, four, eight):
    row = (2 * (eight // 2) + (four >> 1) + core) & 7
    column = (2 * (eight % 2) + (four & 1) + core) & 3
    return row * 4 + column


def device_of(core, four, eight):
    return chip_of(core, four, eight) * 2 + core


EIGHT_GROUPS = [[device_of(core, four, eight) for eight in range(EIGHT)] for core in range(2) for four in range(FOUR)]
SWAP_CORES = [(device, device ^ 1) for device in range(2 * FOUR * EIGHT)]


def four_pairs(step):
    return [
        (device_of(core, four, eight), device_of(core, four ^ step, eight))
        for core in range(2)
        for four in range(FOUR)
        for eight in range(EIGHT)
    ]


def exchange(blocks, axis, groups=None):
    return lax.all_to_all(blocks, axis, 0, 0, axis_index_groups=groups, tiled=True)


def spread(block, count, axis, groups=None):
    return exchange(jnp.broadcast_to(block[None], (count,) + block.shape), axis, groups)


def call(kernel, *out_shapes, mebibytes=16, **specs):
    return pl.pallas_call(
        kernel,
        out_shape=out_shapes,
        **specs,
        compiler_params=pltpu.CompilerParams(vmem_limit_bytes=mebibytes * 1024 * 1024),
    )


def lanes_of(block):
    return slice(block * LANES, (block + 1) * LANES)


def split_kernel(
    tokens_hbm,
    cotangent_hbm,
    weight_hbm,
    gain_ref,
    keep_hbm,
    send_hbm,
    scaled_ref,
    inverse_ref,
    spread_ref,
    tokens_ref,
    cotangent_ref,
    weight_ref,
    keep_ref,
    send_ref,
    in_semaphores,
    out_semaphores,
):
    rows, width = tokens_ref.shape
    pieces = 4
    piece = width // pieces
    copies = [
        pltpu.make_async_copy(weight_hbm, weight_ref, in_semaphores.at[pieces]),
        pltpu.make_async_copy(cotangent_hbm, cotangent_ref, in_semaphores.at[pieces + 1]),
    ]
    for index in range(pieces):
        part = slice(index * piece, (index + 1) * piece)
        copies.append(pltpu.make_async_copy(tokens_hbm.at[:, part], tokens_ref.at[:, part], in_semaphores.at[index]))
    for copy in copies:
        copy.start()

    copies[0].wait()
    gains = jnp.broadcast_to(gain_ref[...].astype(jnp.float32), (LANES, LANES)).T
    scaled_weight = (weight_ref[...].astype(jnp.float32) * gains).astype(jnp.bfloat16)
    for eight in range(EIGHT):
        spread_ref[eight] = scaled_weight

    def squares(index):
        total = jnp.zeros((rows, LANES), jnp.float32)
        for block in range(index * piece // LANES, (index + 1) * piece // LANES):
            floats = tokens_ref[:, lanes_of(block)].astype(jnp.float32)
            total += floats * floats
        return total

    total = jnp.zeros((rows, LANES), jnp.float32)
    for index in range(pieces - 1):
        copies[2 + index].wait()
        total += squares(index)
    copies[1 + pieces].wait()

    device = lax.axis_index("fsdp")
    core, row, column = device & 1, device >> 3, (device >> 1) & 3
    out_copies = []
    for step in range(FOUR):
        part = slice(step * EIGHT * LANES, (step + 1) * EIGHT * LANES)
        for target, target_hbm, kind in ((keep_ref, keep_hbm, core), (send_ref, send_hbm, 1 - core)):
            four = (((row + kind) & 1) * 2 + ((column + kind) & 1)) ^ step
            for eight in range(EIGHT):
                start = pl.multiple_of(device_of(kind, four, eight) * LANES, LANES)
                target[:, lanes_of(step * EIGHT + eight)] = tokens_ref[:, pl.ds(start, LANES)]
            semaphore = out_semaphores.at[len(out_copies)]
            out_copies.append(pltpu.make_async_copy(target.at[:, part], target_hbm.at[:, part], semaphore))
            out_copies[-1].start()

    total += squares(pieces - 1)
    inverse = lax.rsqrt(jnp.sum(total, axis=1, keepdims=True) / width + 1e-05)
    inverse_ref[...] = jnp.broadcast_to(inverse, (rows, LANES))
    copies[1].wait()
    scaled = (cotangent_ref[...].astype(jnp.float32) * inverse).astype(jnp.bfloat16)
    scaled_ref[...] = scaled
    last = lanes_of(FOUR * EIGHT)
    send_ref[:, last] = scaled
    out_copies.append(
        pltpu.make_async_copy(send_ref.at[:, last], send_hbm.at[:, last], out_semaphores.at[len(out_copies)])
    )
    out_copies[-1].start()
    for copy in out_copies:
        copy.wait()


def gradient_term(keep_ref, arrived_ref, scaled_ref, step):
    part = slice(step * EIGHT * LANES, (step + 1) * EIGHT * LANES)
    cotangents = jnp.concatenate([scaled_ref[...], arrived_ref[:, lanes_of(FOUR * EIGHT)]], axis=0)
    both = jnp.concatenate([keep_ref[:, part], arrived_ref[:, part]], axis=0)
    return lax.dot_general(cotangents, both, (((0,), (0,)), ((), ())), preferred_element_type=jnp.float32)


def first_kernel(keep_ref, arrived_ref, scaled_ref, out_ref):
    for index in range(2):
        term = gradient_term(keep_ref, arrived_ref, scaled_ref, ALONG_Y + index)
        for eight in range(EIGHT):
            out_ref[index, eight] = term[:, lanes_of(eight)].astype(jnp.bfloat16)


def second_kernel(keep_ref, arrived_ref, scaled_ref, first_ref, weight_ref, x_weight_ref, out_ref, weights_ref):
    term = gradient_term(keep_ref, arrived_ref, scaled_ref, ALONG_X)
    for eight in range(EIGHT):
        out_ref[eight] = (term[:, lanes_of(eight)] + first_ref[1, eight].astype(jnp.float32)).astype(jnp.bfloat16)
        weights_ref[0, eight] = weight_ref[eight]
        weights_ref[1, eight] = x_weight_ref[eight]


def third_kernel(keep_ref, arrived_ref, scaled_ref, first_ref, second_ref, out_ref):
    term = gradient_term(keep_ref, arrived_ref, scaled_ref, 0)
    for eight in range(EIGHT):
        total = term[:, lanes_of(eight)] + first_ref[0, eight].astype(jnp.float32)
        out_ref[eight] = (total + second_ref[eight].astype(jnp.float32)).astype(jnp.bfloat16)


def values_kernel(keep_ref, arrived_ref, weights_ref, y_weights_ref, own_ref, other_ref):
    columns = EIGHT * LANES
    rows, head = own_ref.shape
    total = jnp.zeros((2 * rows, head), jnp.float32)
    for step in range(FOUR):
        part = slice(step * columns, (step + 1) * columns)
        both = jnp.concatenate([keep_ref[:, part], arrived_ref[:, part]], axis=0)
        weight = (weights_ref, y_weights_ref)[step // 2][step % 2].reshape(columns, head)
        total += jnp.dot(both, weight, preferred_element_type=jnp.float32)
    own_ref[...] = total[:rows]
    other_ref[...] = total[rows:]


def adam_direction(gradient, first_moment, second_moment, first_fix, second_fix):
    first_new = 0.9 * first_moment + 0.1 * gradient
    second_new = 0.95 * second_moment + 0.05 * gradient * gradient
    return first_new / first_fix / (jnp.sqrt(second_new / second_fix) + 1e-08)


def adam_kernel(
    token_total,
    terms_ref,
    weight_ref,
    gain_ref,
    fixes_ref,
    m_weight_ref,
    v_weight_ref,
    m_gain_ref,
    v_gain_ref,
    weight_step_ref,
    gain_step_ref,
):
    total = terms_ref[0].astype(jnp.float32)
    for block in range(1, EIGHT):
        total += terms_ref[block].astype(jnp.float32)
    gradient = total / token_total
    fixes = fixes_ref[0:1, :], fixes_ref[1:2, :]
    weight_gradient = (gradient * gain_ref[...].astype(jnp.float32)).T
    weight_step_ref[...] = adam_direction(weight_gradient, m_weight_ref[...], v_weight_ref[...], *fixes)
    gain_gradient = jnp.sum(gradient * weight_ref[...].astype(jnp.float32).T, axis=0, keepdims=True)
    gain_step_ref[...] = adam_direction(gain_gradient, m_gain_ref[...], v_gain_ref[...], *fixes)


def outer_update(global_params, moment, local_mean):
    delta = global_params - local_mean
    moment_new = 0.9 * moment + delta
    return (global_params - 0.7 * (delta + 0.9 * moment_new), moment_new)


def local(
    tokens_in,
    norm_gain,
    value_weight,
    value_cotangent,
    step_count,
    m_weight,
    v_weight,
    m_gain,
    v_gain,
    frag_local,
    frag_global,
    frag_moment,
):
    rows, width = tokens_in.shape[1:]
    head = value_weight.shape[2]
    half = width // 2
    token_total = rows * lax.axis_size("fsdp")
    replicas = lax.axis_size("rep")
    frag_shape = frag_local.shape[1:]

    hbm = pl.BlockSpec(memory_space=pltpu.HBM)
    keep, send, scaled, inverse_rms, spread_weight = call(
        split_kernel,
        jax.ShapeDtypeStruct((rows, half), jnp.bfloat16),
        jax.ShapeDtypeStruct((rows, half + LANES), jnp.bfloat16),
        jax.ShapeDtypeStruct((rows, head), jnp.bfloat16),
        jax.ShapeDtypeStruct((rows, LANES), jnp.float32),
        jax.ShapeDtypeStruct((EIGHT, LANES, head), jnp.bfloat16),
        mebibytes=60,
        in_specs=[hbm, hbm, hbm, pl.BlockSpec(memory_space=pltpu.VMEM)],
        out_specs=[hbm, hbm] + [pl.BlockSpec(memory_space=pltpu.VMEM)] * 3,
        scratch_shapes=[
            pltpu.VMEM((rows, width), jnp.bfloat16),
            pltpu.VMEM((rows, head), jnp.bfloat16),
            pltpu.VMEM((LANES, head), jnp.bfloat16),
            pltpu.VMEM((rows, half), jnp.bfloat16),
            pltpu.VMEM((rows, half + LANES), jnp.bfloat16),
            pltpu.SemaphoreType.DMA((6,)),
            pltpu.SemaphoreType.DMA((2 * FOUR + 1,)),
        ],
    )(tokens_in[0], value_cotangent[0], value_weight[0], norm_gain)
    arrived = lax.ppermute(send, "fsdp", SWAP_CORES)
    weight = exchange(spread_weight, "fsdp", EIGHT_GROUPS)

    blocks = jax.ShapeDtypeStruct((EIGHT, head, LANES), jnp.bfloat16)
    two_blocks = jax.ShapeDtypeStruct((2, EIGHT, head, LANES), jnp.bfloat16)
    (first,) = call(first_kernel, two_blocks)(keep, arrived, scaled)
    first, weight = lax.optimization_barrier((first, weight))
    first = lax.ppermute(first, "fsdp", four_pairs(ALONG_Y))
    x_weight = lax.ppermute(weight, "fsdp", four_pairs(ALONG_X))

    frag = frag_local[0].astype(jnp.bfloat16).reshape(replicas, -1, frag_shape[1])
    first, frag = lax.optimization_barrier((first, frag))
    frag_terms = exchange(frag, "rep")
    frag_sum = jnp.sum(frag_terms.astype(jnp.float32), axis=0).astype(jnp.bfloat16)

    second, weights = call(second_kernel, blocks, two_blocks)(keep, arrived, scaled, first, weight, x_weight)
    second = lax.ppermute(second, "fsdp", four_pairs(ALONG_X))
    y_weights = lax.ppermute(weights, "fsdp", four_pairs(ALONG_Y))

    local_sum = spread(frag_sum, replicas, "rep")
    (summed,) = call(third_kernel, blocks)(keep, arrived, scaled, first, second)
    summed, local_sum = lax.optimization_barrier((summed, local_sum))
    scattered = exchange(summed, "fsdp", EIGHT_GROUPS)
    local_mean = local_sum.reshape(frag_shape).astype(jnp.float32) / replicas
    new_global, new_moment = outer_update(frag_global, frag_moment, local_mean)
    new_global, keep = lax.optimization_barrier((new_global, keep))

    partial = jax.ShapeDtypeStruct((rows, head), jnp.float32)
    own_part, other_part = call(values_kernel, partial, partial)(keep, arrived, weights, y_weights)
    arrived_part = lax.ppermute(other_part, "fsdp", SWAP_CORES)
    values = ((own_part + arrived_part) * inverse_rms).astype(jnp.bfloat16)

    steps = step_count.astype(jnp.float32)
    fixes = 1.0 - jnp.power(jnp.array([[0.9], [0.95]], jnp.float32), steps)
    weight_step, gain_step = call(
        functools.partial(adam_kernel, token_total),
        jax.ShapeDtypeStruct(m_weight.shape[1:], jnp.float32),
        jax.ShapeDtypeStruct(m_gain.shape, jnp.float32),
    )(
        scattered,
        value_weight[0],
        norm_gain,
        jnp.broadcast_to(fixes, (2, LANES)),
        m_weight[0],
        v_weight[0],
        m_gain,
        v_gain,
    )
    return (values[None], weight_step[None], gain_step, new_global, new_moment)


def solution(mesh):
    in_specs = (
        P("rep", "fsdp", None),
        P("rep", "fsdp"),
        P("rep", "fsdp", None),
        P("rep", "fsdp", None),
        P(),
        P("rep", "fsdp", None),
        P("rep", "fsdp", None),
        P("rep", "fsdp"),
        P("rep", "fsdp"),
        P("rep", "fsdp", None),
        P("fsdp", None),
        P("fsdp", None),
    )
    out_specs = (
        P("rep", "fsdp", None),
        P("rep", "fsdp", None),
        P("rep", "fsdp"),
        P("fsdp", None),
        P("fsdp", None),
    )
    return jax.shard_map(local, mesh=mesh, in_specs=in_specs, out_specs=out_specs, check_vma=False)
```

```python
import functools

import jax
import jax.numpy as jnp
from jax import lax
from jax.experimental import pallas as pl
from jax.experimental.pallas import tpu as pltpu
from jax.sharding import PartitionSpec as P

EIGHT = 8
FOUR = 4
ALONG_X, ALONG_Y = 1, 2
LANES = 128


def chip_of(core, four, eight):
    row = (2 * (eight // 2) + (four >> 1) + core) & 7
    column = (2 * (eight % 2) + (four & 1) + core) & 3
    return row * 4 + column


def device_of(core, four, eight):
    return chip_of(core, four, eight) * 2 + core


EIGHT_GROUPS = [[device_of(core, four, eight) for eight in range(EIGHT)] for core in range(2) for four in range(FOUR)]
SWAP_CORES = [(device, device ^ 1) for device in range(2 * FOUR * EIGHT)]


def four_pairs(step):
    return [
        (device_of(core, four, eight), device_of(core, four ^ step, eight))
        for core in range(2)
        for four in range(FOUR)
        for eight in range(EIGHT)
    ]


def exchange(blocks, axis, groups=None):
    return lax.all_to_all(blocks, axis, 0, 0, axis_index_groups=groups, tiled=True)


def spread(block, count, axis, groups=None):
    return exchange(jnp.broadcast_to(block[None], (count,) + block.shape), axis, groups)


def call(kernel, *out_shapes, mebibytes=16, **specs):
    return pl.pallas_call(
        kernel,
        out_shape=out_shapes,
        **specs,
        compiler_params=pltpu.CompilerParams(vmem_limit_bytes=mebibytes * 1024 * 1024),
    )


def lanes_of(block):
    return slice(block * LANES, (block + 1) * LANES)


def split_kernel(
    tokens_hbm,
    cotangent_hbm,
    weight_hbm,
    gain_ref,
    keep_hbm,
    send_hbm,
    scaled_ref,
    inverse_ref,
    spread_ref,
    tokens_ref,
    cotangent_ref,
    weight_ref,
    keep_ref,
    send_ref,
    in_semaphores,
    out_semaphores,
):
    rows, width = tokens_ref.shape
    pieces = 4
    piece = width // pieces
    copies = [
        pltpu.make_async_copy(weight_hbm, weight_ref, in_semaphores.at[pieces]),
        pltpu.make_async_copy(cotangent_hbm, cotangent_ref, in_semaphores.at[pieces + 1]),
    ]
    for index in range(pieces):
        part = slice(index * piece, (index + 1) * piece)
        copies.append(pltpu.make_async_copy(tokens_hbm.at[:, part], tokens_ref.at[:, part], in_semaphores.at[index]))
    for copy in copies:
        copy.start()

    copies[0].wait()
    gains = jnp.broadcast_to(gain_ref[...].astype(jnp.float32), (LANES, LANES)).T
    scaled_weight = (weight_ref[...].astype(jnp.float32) * gains).astype(jnp.bfloat16)
    for eight in range(EIGHT):
        spread_ref[eight] = scaled_weight

    def squares(index):
        total = jnp.zeros((rows, LANES), jnp.float32)
        for block in range(index * piece // LANES, (index + 1) * piece // LANES):
            floats = tokens_ref[:, lanes_of(block)].astype(jnp.float32)
            total += floats * floats
        return total

    total = jnp.zeros((rows, LANES), jnp.float32)
    for index in range(pieces - 1):
        copies[2 + index].wait()
        total += squares(index)
    copies[1 + pieces].wait()

    device = lax.axis_index("fsdp")
    core, row, column = device & 1, device >> 3, (device >> 1) & 3
    out_copies = []
    for step in range(FOUR):
        part = slice(step * EIGHT * LANES, (step + 1) * EIGHT * LANES)
        for target, target_hbm, kind in ((keep_ref, keep_hbm, core), (send_ref, send_hbm, 1 - core)):
            four = (((row + kind) & 1) * 2 + ((column + kind) & 1)) ^ step
            for eight in range(EIGHT):
                start = pl.multiple_of(device_of(kind, four, eight) * LANES, LANES)
                target[:, lanes_of(step * EIGHT + eight)] = tokens_ref[:, pl.ds(start, LANES)]
            semaphore = out_semaphores.at[len(out_copies)]
            out_copies.append(pltpu.make_async_copy(target.at[:, part], target_hbm.at[:, part], semaphore))
            out_copies[-1].start()

    total += squares(pieces - 1)
    inverse = lax.rsqrt(jnp.sum(total, axis=1, keepdims=True) / width + 1e-05)
    inverse_ref[...] = jnp.broadcast_to(inverse, (rows, LANES))
    copies[1].wait()
    scaled = (cotangent_ref[...].astype(jnp.float32) * inverse).astype(jnp.bfloat16)
    scaled_ref[...] = scaled
    last = lanes_of(FOUR * EIGHT)
    send_ref[:, last] = scaled
    out_copies.append(
        pltpu.make_async_copy(send_ref.at[:, last], send_hbm.at[:, last], out_semaphores.at[len(out_copies)])
    )
    out_copies[-1].start()
    for copy in out_copies:
        copy.wait()


def gradient_term(keep_ref, arrived_ref, scaled_ref, step):
    part = slice(step * EIGHT * LANES, (step + 1) * EIGHT * LANES)
    cotangents = jnp.concatenate([scaled_ref[...], arrived_ref[:, lanes_of(FOUR * EIGHT)]], axis=0)
    both = jnp.concatenate([keep_ref[:, part], arrived_ref[:, part]], axis=0)
    return lax.dot_general(cotangents, both, (((0,), (0,)), ((), ())), preferred_element_type=jnp.float32)


def first_kernel(keep_ref, arrived_ref, scaled_ref, out_ref):
    for index in range(2):
        term = gradient_term(keep_ref, arrived_ref, scaled_ref, ALONG_Y + index)
        for eight in range(EIGHT):
            out_ref[index, eight] = term[:, lanes_of(eight)].astype(jnp.bfloat16)


def second_kernel(keep_ref, arrived_ref, scaled_ref, first_ref, out_ref):
    term = gradient_term(keep_ref, arrived_ref, scaled_ref, ALONG_X)
    for eight in range(EIGHT):
        out_ref[eight] = (term[:, lanes_of(eight)] + first_ref[1, eight].astype(jnp.float32)).astype(jnp.bfloat16)


def join_kernel(weight_ref, x_weight_ref, out_ref):
    out_ref[0] = weight_ref[...]
    out_ref[1] = x_weight_ref[...]


def third_kernel(keep_ref, arrived_ref, scaled_ref, first_ref, second_ref, out_ref):
    term = gradient_term(keep_ref, arrived_ref, scaled_ref, 0)
    for eight in range(EIGHT):
        total = term[:, lanes_of(eight)] + first_ref[0, eight].astype(jnp.float32)
        out_ref[eight] = (total + second_ref[eight].astype(jnp.float32)).astype(jnp.bfloat16)


def values_kernel(keep_ref, arrived_ref, weights_ref, y_weights_ref, own_ref, other_ref):
    columns = EIGHT * LANES
    rows, head = own_ref.shape
    total = jnp.zeros((2 * rows, head), jnp.float32)
    for step in range(FOUR):
        part = slice(step * columns, (step + 1) * columns)
        both = jnp.concatenate([keep_ref[:, part], arrived_ref[:, part]], axis=0)
        weight = (weights_ref, y_weights_ref)[step // 2][step % 2].reshape(columns, head)
        total += jnp.dot(both, weight, preferred_element_type=jnp.float32)
    own_ref[...] = total[:rows]
    other_ref[...] = total[rows:]


def adam_direction(gradient, first_moment, second_moment, first_fix, second_fix):
    first_new = 0.9 * first_moment + 0.1 * gradient
    second_new = 0.95 * second_moment + 0.05 * gradient * gradient
    return first_new / first_fix / (jnp.sqrt(second_new / second_fix) + 1e-08)


def adam_kernel(
    token_total,
    terms_ref,
    weight_ref,
    gain_ref,
    fixes_ref,
    m_weight_ref,
    v_weight_ref,
    m_gain_ref,
    v_gain_ref,
    weight_step_ref,
    gain_step_ref,
):
    total = terms_ref[0].astype(jnp.float32)
    for block in range(1, EIGHT):
        total += terms_ref[block].astype(jnp.float32)
    gradient = total / token_total
    fixes = fixes_ref[0:1, :], fixes_ref[1:2, :]
    weight_gradient = (gradient * gain_ref[...].astype(jnp.float32)).T
    weight_step_ref[...] = adam_direction(weight_gradient, m_weight_ref[...], v_weight_ref[...], *fixes)
    gain_gradient = jnp.sum(gradient * weight_ref[...].astype(jnp.float32).T, axis=0, keepdims=True)
    gain_step_ref[...] = adam_direction(gain_gradient, m_gain_ref[...], v_gain_ref[...], *fixes)


def outer_update(global_params, moment, local_mean):
    delta = global_params - local_mean
    moment_new = 0.9 * moment + delta
    return (global_params - 0.7 * (delta + 0.9 * moment_new), moment_new)


def local(
    tokens_in,
    norm_gain,
    value_weight,
    value_cotangent,
    step_count,
    m_weight,
    v_weight,
    m_gain,
    v_gain,
    frag_local,
    frag_global,
    frag_moment,
):
    rows, width = tokens_in.shape[1:]
    head = value_weight.shape[2]
    half = width // 2
    token_total = rows * lax.axis_size("fsdp")
    replicas = lax.axis_size("rep")
    frag_shape = frag_local.shape[1:]

    hbm = pl.BlockSpec(memory_space=pltpu.HBM)
    keep, send, scaled, inverse_rms, spread_weight = call(
        split_kernel,
        jax.ShapeDtypeStruct((rows, half), jnp.bfloat16),
        jax.ShapeDtypeStruct((rows, half + LANES), jnp.bfloat16),
        jax.ShapeDtypeStruct((rows, head), jnp.bfloat16),
        jax.ShapeDtypeStruct((rows, LANES), jnp.float32),
        jax.ShapeDtypeStruct((EIGHT, LANES, head), jnp.bfloat16),
        mebibytes=60,
        in_specs=[hbm, hbm, hbm, pl.BlockSpec(memory_space=pltpu.VMEM)],
        out_specs=[hbm, hbm] + [pl.BlockSpec(memory_space=pltpu.VMEM)] * 3,
        scratch_shapes=[
            pltpu.VMEM((rows, width), jnp.bfloat16),
            pltpu.VMEM((rows, head), jnp.bfloat16),
            pltpu.VMEM((LANES, head), jnp.bfloat16),
            pltpu.VMEM((rows, half), jnp.bfloat16),
            pltpu.VMEM((rows, half + LANES), jnp.bfloat16),
            pltpu.SemaphoreType.DMA((6,)),
            pltpu.SemaphoreType.DMA((2 * FOUR + 1,)),
        ],
    )(tokens_in[0], value_cotangent[0], value_weight[0], norm_gain)
    arrived = lax.ppermute(send, "fsdp", SWAP_CORES)
    frag = frag_local[0].astype(jnp.bfloat16).reshape(replicas, -1, frag_shape[1])
    frag_terms = exchange(frag, "rep")

    blocks = jax.ShapeDtypeStruct((EIGHT, head, LANES), jnp.bfloat16)
    two_blocks = jax.ShapeDtypeStruct((2, EIGHT, head, LANES), jnp.bfloat16)
    (first,) = call(first_kernel, two_blocks, mebibytes=16)(keep, arrived, scaled)
    first = lax.ppermute(first, "fsdp", four_pairs(ALONG_Y))
    frag_terms, spread_weight = lax.optimization_barrier((frag_terms, spread_weight))
    weight = exchange(spread_weight, "fsdp", EIGHT_GROUPS)
    (second,) = call(second_kernel, blocks)(keep, arrived, scaled, first)
    second = lax.ppermute(second, "fsdp", four_pairs(ALONG_X))
    x_weight = lax.ppermute(weight, "fsdp", four_pairs(ALONG_X))
    (weights,) = call(join_kernel, two_blocks)(weight, x_weight)
    y_weights = lax.ppermute(weights, "fsdp", four_pairs(ALONG_Y))
    frag_sum = jnp.sum(frag_terms.astype(jnp.float32), axis=0).astype(jnp.bfloat16)
    local_sum = spread(frag_sum, replicas, "rep")

    (summed,) = call(third_kernel, blocks)(keep, arrived, scaled, first, second)
    summed, local_sum = lax.optimization_barrier((summed, local_sum))
    scattered = exchange(summed, "fsdp", EIGHT_GROUPS)
    local_mean = local_sum.reshape(frag_shape).astype(jnp.float32) / replicas
    new_global, new_moment = outer_update(frag_global, frag_moment, local_mean)
    new_global, keep = lax.optimization_barrier((new_global, keep))

    partial = jax.ShapeDtypeStruct((rows, head), jnp.float32)
    own_part, other_part = call(values_kernel, partial, partial)(keep, arrived, weights, y_weights)
    arrived_part = lax.ppermute(other_part, "fsdp", SWAP_CORES)
    values = ((own_part + arrived_part) * inverse_rms).astype(jnp.bfloat16)

    steps = step_count.astype(jnp.float32)
    fixes = 1.0 - jnp.power(jnp.array([[0.9], [0.95]], jnp.float32), steps)
    weight_step, gain_step = call(
        functools.partial(adam_kernel, token_total),
        jax.ShapeDtypeStruct(m_weight.shape[1:], jnp.float32),
        jax.ShapeDtypeStruct(m_gain.shape, jnp.float32),
    )(
        scattered,
        value_weight[0],
        norm_gain,
        jnp.broadcast_to(fixes, (2, LANES)),
        m_weight[0],
        v_weight[0],
        m_gain,
        v_gain,
    )
    return (values[None], weight_step[None], gain_step, new_global, new_moment)


def solution(mesh):
    in_specs = (
        P("rep", "fsdp", None),
        P("rep", "fsdp"),
        P("rep", "fsdp", None),
        P("rep", "fsdp", None),
        P(),
        P("rep", "fsdp", None),
        P("rep", "fsdp", None),
        P("rep", "fsdp"),
        P("rep", "fsdp"),
        P("rep", "fsdp", None),
        P("fsdp", None),
        P("fsdp", None),
    )
    out_specs = (
        P("rep", "fsdp", None),
        P("rep", "fsdp", None),
        P("rep", "fsdp"),
        P("fsdp", None),
        P("fsdp", None),
    )
    return jax.shard_map(local, mesh=mesh, in_specs=in_specs, out_specs=out_specs, check_vma=False)
```

```python
import functools

import jax
import jax.numpy as jnp
from jax import lax
from jax.experimental import pallas as pl
from jax.experimental.pallas import tpu as pltpu
from jax.sharding import PartitionSpec as P

EIGHT = 8
FOUR = 4
ALONG_X, ALONG_Y = 1, 2
LANES = 128


def chip_of(core, four, eight):
    row = (2 * (eight // 2) + (four >> 1) + core) & 7
    column = (2 * (eight % 2) + (four & 1) + core) & 3
    return row * 4 + column


def device_of(core, four, eight):
    return chip_of(core, four, eight) * 2 + core


EIGHT_GROUPS = [[device_of(core, four, eight) for eight in range(EIGHT)] for core in range(2) for four in range(FOUR)]
SWAP_CORES = [(device, device ^ 1) for device in range(2 * FOUR * EIGHT)]


def four_pairs(step):
    return [
        (device_of(core, four, eight), device_of(core, four ^ step, eight))
        for core in range(2)
        for four in range(FOUR)
        for eight in range(EIGHT)
    ]


def exchange(blocks, axis, groups=None):
    return lax.all_to_all(blocks, axis, 0, 0, axis_index_groups=groups, tiled=True)


def spread(block, count, axis, groups=None):
    return exchange(jnp.broadcast_to(block[None], (count,) + block.shape), axis, groups)


def call(kernel, *out_shapes, mebibytes=16, **specs):
    return pl.pallas_call(
        kernel,
        out_shape=out_shapes,
        **specs,
        compiler_params=pltpu.CompilerParams(vmem_limit_bytes=mebibytes * 1024 * 1024),
    )


def lanes_of(block):
    return slice(block * LANES, (block + 1) * LANES)


def split_kernel(
    tokens_hbm,
    cotangent_hbm,
    weight_hbm,
    gain_ref,
    keep_hbm,
    send_hbm,
    scaled_ref,
    inverse_ref,
    spread_ref,
    tokens_ref,
    cotangent_ref,
    weight_ref,
    keep_ref,
    send_ref,
    in_semaphores,
    out_semaphores,
):
    rows, width = tokens_ref.shape
    pieces = 4
    piece = width // pieces
    copies = [
        pltpu.make_async_copy(weight_hbm, weight_ref, in_semaphores.at[pieces]),
        pltpu.make_async_copy(cotangent_hbm, cotangent_ref, in_semaphores.at[pieces + 1]),
    ]
    for index in range(pieces):
        part = slice(index * piece, (index + 1) * piece)
        copies.append(pltpu.make_async_copy(tokens_hbm.at[:, part], tokens_ref.at[:, part], in_semaphores.at[index]))
    for copy in copies:
        copy.start()

    copies[0].wait()
    gains = jnp.broadcast_to(gain_ref[...].astype(jnp.float32), (LANES, LANES)).T
    scaled_weight = (weight_ref[...].astype(jnp.float32) * gains).astype(jnp.bfloat16)
    for eight in range(EIGHT):
        spread_ref[eight] = scaled_weight

    def squares(index):
        total = jnp.zeros((rows, LANES), jnp.float32)
        for block in range(index * piece // LANES, (index + 1) * piece // LANES):
            floats = tokens_ref[:, lanes_of(block)].astype(jnp.float32)
            total += floats * floats
        return total

    total = jnp.zeros((rows, LANES), jnp.float32)
    for index in range(pieces - 1):
        copies[2 + index].wait()
        total += squares(index)
    copies[1 + pieces].wait()

    device = lax.axis_index("fsdp")
    core, row, column = device & 1, device >> 3, (device >> 1) & 3
    out_copies = []
    for step in range(FOUR):
        part = slice(step * EIGHT * LANES, (step + 1) * EIGHT * LANES)
        for target, target_hbm, kind in ((keep_ref, keep_hbm, core), (send_ref, send_hbm, 1 - core)):
            four = (((row + kind) & 1) * 2 + ((column + kind) & 1)) ^ step
            for eight in range(EIGHT):
                start = pl.multiple_of(device_of(kind, four, eight) * LANES, LANES)
                target[:, lanes_of(step * EIGHT + eight)] = tokens_ref[:, pl.ds(start, LANES)]
            semaphore = out_semaphores.at[len(out_copies)]
            out_copies.append(pltpu.make_async_copy(target.at[:, part], target_hbm.at[:, part], semaphore))
            out_copies[-1].start()

    total += squares(pieces - 1)
    inverse = lax.rsqrt(jnp.sum(total, axis=1, keepdims=True) / width + 1e-05)
    inverse_ref[...] = jnp.broadcast_to(inverse, (rows, LANES))
    copies[1].wait()
    scaled = (cotangent_ref[...].astype(jnp.float32) * inverse).astype(jnp.bfloat16)
    scaled_ref[...] = scaled
    last = lanes_of(FOUR * EIGHT)
    send_ref[:, last] = scaled
    out_copies.append(
        pltpu.make_async_copy(send_ref.at[:, last], send_hbm.at[:, last], out_semaphores.at[len(out_copies)])
    )
    out_copies[-1].start()
    for copy in out_copies:
        copy.wait()


def gradient_term(keep_ref, arrived_ref, scaled_ref, step):
    part = slice(step * EIGHT * LANES, (step + 1) * EIGHT * LANES)
    cotangents = jnp.concatenate([scaled_ref[...], arrived_ref[:, lanes_of(FOUR * EIGHT)]], axis=0)
    both = jnp.concatenate([keep_ref[:, part], arrived_ref[:, part]], axis=0)
    return lax.dot_general(cotangents, both, (((0,), (0,)), ((), ())), preferred_element_type=jnp.float32)


def first_kernel(keep_ref, arrived_ref, scaled_ref, out_ref):
    for index in range(2):
        term = gradient_term(keep_ref, arrived_ref, scaled_ref, ALONG_Y + index)
        for eight in range(EIGHT):
            out_ref[index, eight] = term[:, lanes_of(eight)].astype(jnp.bfloat16)


def second_kernel(keep_ref, arrived_ref, scaled_ref, first_ref, out_ref):
    term = gradient_term(keep_ref, arrived_ref, scaled_ref, ALONG_X)
    for eight in range(EIGHT):
        out_ref[eight] = (term[:, lanes_of(eight)] + first_ref[1, eight].astype(jnp.float32)).astype(jnp.bfloat16)


def join_kernel(weight_ref, x_weight_ref, out_ref):
    out_ref[0] = weight_ref[...]
    out_ref[1] = x_weight_ref[...]


def third_kernel(keep_ref, arrived_ref, scaled_ref, first_ref, second_ref, out_ref):
    term = gradient_term(keep_ref, arrived_ref, scaled_ref, 0)
    for eight in range(EIGHT):
        total = term[:, lanes_of(eight)] + first_ref[0, eight].astype(jnp.float32)
        out_ref[eight] = (total + second_ref[eight].astype(jnp.float32)).astype(jnp.bfloat16)


def values_kernel(keep_ref, arrived_ref, weights_ref, y_weights_ref, own_ref, other_ref):
    columns = EIGHT * LANES
    rows, head = own_ref.shape
    total = jnp.zeros((2 * rows, head), jnp.float32)
    for step in range(FOUR):
        part = slice(step * columns, (step + 1) * columns)
        both = jnp.concatenate([keep_ref[:, part], arrived_ref[:, part]], axis=0)
        weight = (weights_ref, y_weights_ref)[step // 2][step % 2].reshape(columns, head)
        total += jnp.dot(both, weight, preferred_element_type=jnp.float32)
    own_ref[...] = total[:rows]
    other_ref[...] = total[rows:]


def adam_direction(gradient, first_moment, second_moment, first_fix, second_fix):
    first_new = 0.9 * first_moment + 0.1 * gradient
    second_new = 0.95 * second_moment + 0.05 * gradient * gradient
    return first_new / first_fix / (jnp.sqrt(second_new / second_fix) + 1e-08)


def adam_kernel(
    token_total,
    terms_ref,
    weight_ref,
    gain_ref,
    fixes_ref,
    m_weight_ref,
    v_weight_ref,
    m_gain_ref,
    v_gain_ref,
    weight_step_ref,
    gain_step_ref,
):
    total = terms_ref[0].astype(jnp.float32)
    for block in range(1, EIGHT):
        total += terms_ref[block].astype(jnp.float32)
    gradient = total / token_total
    fixes = fixes_ref[0:1, :], fixes_ref[1:2, :]
    weight_gradient = (gradient * gain_ref[...].astype(jnp.float32)).T
    weight_step_ref[...] = adam_direction(weight_gradient, m_weight_ref[...], v_weight_ref[...], *fixes)
    gain_gradient = jnp.sum(gradient * weight_ref[...].astype(jnp.float32).T, axis=0, keepdims=True)
    gain_step_ref[...] = adam_direction(gain_gradient, m_gain_ref[...], v_gain_ref[...], *fixes)


def outer_update(global_params, moment, local_mean):
    delta = global_params - local_mean
    moment_new = 0.9 * moment + delta
    return (global_params - 0.7 * (delta + 0.9 * moment_new), moment_new)


def local(
    tokens_in,
    norm_gain,
    value_weight,
    value_cotangent,
    step_count,
    m_weight,
    v_weight,
    m_gain,
    v_gain,
    frag_local,
    frag_global,
    frag_moment,
):
    rows, width = tokens_in.shape[1:]
    head = value_weight.shape[2]
    half = width // 2
    token_total = rows * lax.axis_size("fsdp")
    replicas = lax.axis_size("rep")
    frag_shape = frag_local.shape[1:]

    hbm = pl.BlockSpec(memory_space=pltpu.HBM)
    keep, send, scaled, inverse_rms, spread_weight = call(
        split_kernel,
        jax.ShapeDtypeStruct((rows, half), jnp.bfloat16),
        jax.ShapeDtypeStruct((rows, half + LANES), jnp.bfloat16),
        jax.ShapeDtypeStruct((rows, head), jnp.bfloat16),
        jax.ShapeDtypeStruct((rows, LANES), jnp.float32),
        jax.ShapeDtypeStruct((EIGHT, LANES, head), jnp.bfloat16),
        mebibytes=60,
        in_specs=[hbm, hbm, hbm, pl.BlockSpec(memory_space=pltpu.VMEM)],
        out_specs=[hbm, hbm] + [pl.BlockSpec(memory_space=pltpu.VMEM)] * 3,
        scratch_shapes=[
            pltpu.VMEM((rows, width), jnp.bfloat16),
            pltpu.VMEM((rows, head), jnp.bfloat16),
            pltpu.VMEM((LANES, head), jnp.bfloat16),
            pltpu.VMEM((rows, half), jnp.bfloat16),
            pltpu.VMEM((rows, half + LANES), jnp.bfloat16),
            pltpu.SemaphoreType.DMA((6,)),
            pltpu.SemaphoreType.DMA((2 * FOUR + 1,)),
        ],
    )(tokens_in[0], value_cotangent[0], value_weight[0], norm_gain)
    arrived = lax.ppermute(send, "fsdp", SWAP_CORES)
    frag = frag_local[0].astype(jnp.bfloat16).reshape(replicas, -1, frag_shape[1])
    frag_terms = exchange(frag, "rep")

    blocks = jax.ShapeDtypeStruct((EIGHT, head, LANES), jnp.bfloat16)
    two_blocks = jax.ShapeDtypeStruct((2, EIGHT, head, LANES), jnp.bfloat16)
    (first,) = call(first_kernel, two_blocks, mebibytes=16)(keep, arrived, scaled)
    first = lax.ppermute(first, "fsdp", four_pairs(ALONG_Y))
    frag_terms, spread_weight = lax.optimization_barrier((frag_terms, spread_weight))
    weight = exchange(spread_weight, "fsdp", EIGHT_GROUPS)
    (second,) = call(second_kernel, blocks)(keep, arrived, scaled, first)
    second = lax.ppermute(second, "fsdp", four_pairs(ALONG_X))
    x_weight = lax.ppermute(weight, "fsdp", four_pairs(ALONG_X))
    (weights,) = call(join_kernel, two_blocks)(weight, x_weight)
    y_weights = lax.ppermute(weights, "fsdp", four_pairs(ALONG_Y))
    frag_sum = jnp.sum(frag_terms.astype(jnp.float32), axis=0).astype(jnp.bfloat16)
    second, frag_sum = lax.optimization_barrier((second, frag_sum))
    local_sum = spread(frag_sum, replicas, "rep")

    (summed,) = call(third_kernel, blocks)(keep, arrived, scaled, first, second)
    summed, local_sum = lax.optimization_barrier((summed, local_sum))
    scattered = exchange(summed, "fsdp", EIGHT_GROUPS)
    local_mean = local_sum.reshape(frag_shape).astype(jnp.float32) / replicas
    new_global, new_moment = outer_update(frag_global, frag_moment, local_mean)
    new_global, keep = lax.optimization_barrier((new_global, keep))

    partial = jax.ShapeDtypeStruct((rows, head), jnp.float32)
    own_part, other_part = call(values_kernel, partial, partial)(keep, arrived, weights, y_weights)
    arrived_part = lax.ppermute(other_part, "fsdp", SWAP_CORES)
    values = ((own_part + arrived_part) * inverse_rms).astype(jnp.bfloat16)

    steps = step_count.astype(jnp.float32)
    fixes = 1.0 - jnp.power(jnp.array([[0.9], [0.95]], jnp.float32), steps)
    weight_step, gain_step = call(
        functools.partial(adam_kernel, token_total),
        jax.ShapeDtypeStruct(m_weight.shape[1:], jnp.float32),
        jax.ShapeDtypeStruct(m_gain.shape, jnp.float32),
    )(
        scattered,
        value_weight[0],
        norm_gain,
        jnp.broadcast_to(fixes, (2, LANES)),
        m_weight[0],
        v_weight[0],
        m_gain,
        v_gain,
    )
    return (values[None], weight_step[None], gain_step, new_global, new_moment)


def solution(mesh):
    in_specs = (
        P("rep", "fsdp", None),
        P("rep", "fsdp"),
        P("rep", "fsdp", None),
        P("rep", "fsdp", None),
        P(),
        P("rep", "fsdp", None),
        P("rep", "fsdp", None),
        P("rep", "fsdp"),
        P("rep", "fsdp"),
        P("rep", "fsdp", None),
        P("fsdp", None),
        P("fsdp", None),
    )
    out_specs = (
        P("rep", "fsdp", None),
        P("rep", "fsdp", None),
        P("rep", "fsdp"),
        P("fsdp", None),
        P("fsdp", None),
    )
    return jax.shard_map(local, mesh=mesh, in_specs=in_specs, out_specs=out_specs, check_vma=False)
```
